128 devices in a mesh: grp: 16 (over y, x_hi, core), shard: 8 (over z, x_lo).
Axes of the slice: x: 4 (x_hi: 2, x_lo: 2; x = x_hi * 2 + x_lo), y: 4, z: 4, core: 2. Of those that a mesh axis runs over, the one named last changes fastest.
Arguments:
- left_table: float32 [524288, 400], P(('grp', 'shard')), may hold values from -2.4 to 2.4
- right_table: float32 [524288, 400], P(('grp', 'shard')), may hold values from -2.4 to 2.4
- left_state: float32 [524288], P(('grp', 'shard')), may hold values from 0.1 to 4
- right_state: float32 [524288], P(('grp', 'shard')), may hold values from 0.1 to 4
- relations: float32 [1345, 400], replicated, may hold values from -4.2 to 4.2
- relation_state: float32 [1345], replicated, may hold values from 0.1 to 100000
- source_rows: int32 [1152, 1000], P(('grp', 'shard')), may hold values from 0 to 4095
- relation_ids: int32 [1152, 1000], P(('grp', 'shard')), may hold values from 0 to 1344
- target_rows: int32 [1152, 1000], P(('grp', 'shard')), may hold values from 0 to 4095
- negative_rows: int32 [1152, 1000], P(('grp', 'shard')), may hold values from 0 to 4095
- span_sizes: int32 [128, 9], P(('grp', 'shard')), may hold values from 1 to 1000, 6750 in all within a row
Outputs:
- new_left: float32 [524288, 400], P(('grp', 'shard'))
- new_left_state: float32 [524288], P(('grp', 'shard'))
- new_right: float32 [524288, 400], P(('grp', 'shard'))
- new_right_state: float32 [524288], P(('grp', 'shard'))
- new_relations: float32 [1345, 400], replicated
- new_relation_state: float32 [1345], replicated
The draws below stay inside these ranges and needn't reach their ends.
Inputs may be any that keep to these rules, and one draw needn't show every extreme that they name: `source_rows`: local row ids of the device's own source-side rows. `target_rows`: local row ids of the device's own target-side rows. `negative_rows`: negative j of a span names a local row of device j // 125 of the same group; rows may repeat. The first span_sizes edges of a span are live.
All inputs are finite; a program needn't handle non-finite values.
Results may differ from the reference program's by a relative error of at most 0.0017.
Values may be sent and summed in bfloat16 or wider, within the bound.
A program may use at most 256 MiB of HBM per device.

```python
import math
import jax
import jax.numpy as jnp
import numpy as np
from jax import lax

D = 400
REL = 1345
ROWS_DEV = 4096
SPANS = 9
SPAN = 1000
NEG = 1000
ROUND = 5
NEG_PER = 125
ENT = 524288
NCH = 1152
N_GRP = 16
N_SHARD = 8
DEVICES = 128


def set_ends(values, rng, low, top_value):
    longest = values.shape.index(max(values.shape))
    spots = []
    for shift in (0, 1):
        where = [jax.random.randint(jax.random.fold_in(rng, axis), (), 0, length) for axis, length in enumerate(values.shape)]
        where[longest] = (where[longest] + shift) % values.shape[longest]
        spots.append(tuple(where))
    return values.at[spots[0]].set(low).at[spots[1]].set(top_value)


def shard_levels(key, shape, cuts, low, top_value):
    def one(position, shards_of):
        steps = jax.random.uniform(jax.random.fold_in(jax.random.fold_in(key, 6), position), (shards_of,), jnp.float32, low / len(cuts), top_value / len(cuts))
        return jnp.repeat(jnp.exp(steps), shape[position] // shards_of).reshape((-1,) + (1,) * (len(shape) - position - 1))

    gain = one(*cuts[0])
    for cut in cuts[1:]:
        gain = gain * one(*cut)
    return gain


def cumulative_ranks(amount, lean):
    weights = [(1 << 20) // math.isqrt(standing ** lean) + 1 for standing in range(1, amount + 1)]
    spread = 1 + sum(weights) // (1 << 30)
    return np.cumsum(np.array([max(1, weight // spread) for weight in weights]))


def ranked(rng, extent, number_of, slope):
    listing = cumulative_ranks(number_of, slope)
    ticket = jax.random.randint(jax.random.fold_in(rng, 1), extent, 0, int(listing[number_of - 1]))
    rank = jnp.searchsorted(jnp.asarray(listing, jnp.int32), ticket, side="right")
    return jax.random.permutation(jax.random.fold_in(rng, 2), number_of)[rank].astype(jnp.int32)


def split_up(amount, total, most, lean):
    portions = [(1 << 20) // math.isqrt(rank ** lean) + 1 for rank in range(2, amount + 1)]
    rest, holding = total - most - (amount - 1), [1] * (amount - 1)
    while rest > 0:
        free = [i for i in range(amount - 1) if holding[i] < most]
        pool, left = sum([portions[i] for i in free]), rest
        for i in free:
            more = min(most - holding[i], max(1, left * portions[i] // pool), rest)
            holding[i] = holding[i] + more
            rest = rest - more
    return np.array([most] + holding)


def ragged_sizes(rng, amount, total, reach, skew):
    if amount == 2:
        one = jax.random.randint(rng, (), max(1, total - reach), min(reach, total - 1) + 1)
        return jnp.stack([one, total - one])
    sizes = jnp.asarray(split_up(amount, total, reach, skew), jnp.int32)
    twos = (amount - 1) // 2
    giver, receiver = sizes[1:1 + 2 * twos:2], sizes[2:2 + 2 * twos:2]
    slack = jnp.minimum(giver - 1, reach - receiver)
    passed = jax.random.randint(jax.random.fold_in(rng, 1), (twos,), 0, 1 << 20) % (slack + 1)
    sizes = sizes.at[1:1 + 2 * twos:2].set(giver - passed).at[2:2 + 2 * twos:2].set(receiver + passed)
    return sizes[jax.random.permutation(jax.random.fold_in(rng, 2), amount)]


def gaussian(key, dims, spread, bound, shards=(), kind=jnp.bfloat16):
    loudness = shard_levels(key, dims, shards, -0.22, 0.18) if shards else 1.0
    values = jax.random.normal(key, dims, jnp.float32) * spread * loudness
    return jnp.minimum(jnp.maximum(values, -bound), bound).astype(kind)


def setup_inputs(seed: int = 0) -> dict:
    splits = jax.random.split(jax.random.key(seed), 12)
    return {
        "left_table": gaussian(splits[0], (ENT, D), 0.4, 2.4, ((0, 128),), jnp.float32),
        "right_table": gaussian(splits[1], (ENT, D), 0.4, 2.4, ((0, 128),), jnp.float32),
        "left_state": jnp.clip(jnp.exp(math.log(4.0) - 3.6888794 * jax.random.uniform(splits[2], (ENT,), jnp.float32) ** shard_levels(splits[2], (ENT,), ((0, 128),), -0.2, 0.2)), 0.1, 4.0),
        "right_state": jnp.clip(jnp.exp(math.log(4.0) - 3.6888794 * jax.random.uniform(splits[3], (ENT,), jnp.float32) ** shard_levels(splits[3], (ENT,), ((0, 128),), -0.2, 0.2)), 0.1, 4.0),
        "relations": gaussian(splits[4], (REL, D), 0.7, 4.2, (), jnp.float32),
        "relation_state": jnp.clip(jnp.exp(jax.random.uniform(splits[5], (REL,), jnp.float32, math.log(0.1), math.log(100000.0))), 0.1, 100000.0),
        "source_rows": set_ends(jax.random.randint(splits[6], (NCH, SPAN), 0, ROWS_DEV), jax.random.fold_in(splits[6], 1), 0, ROWS_DEV - 1).astype(jnp.int32),
        "relation_ids": set_ends(ranked(splits[7], (NCH, SPAN), REL, 2), jax.random.fold_in(splits[7], 3), 0, REL - 1).astype(jnp.int32),
        "target_rows": set_ends(jax.random.randint(splits[8], (NCH, SPAN), 0, ROWS_DEV), jax.random.fold_in(splits[8], 1), 0, ROWS_DEV - 1).astype(jnp.int32),
        "negative_rows": set_ends(jax.random.randint(splits[9], (NCH, NEG), 0, ROWS_DEV), jax.random.fold_in(splits[9], 1), 0, ROWS_DEV - 1).astype(jnp.int32),
        "span_sizes": jax.vmap(lambda own: ragged_sizes(own, SPANS, SPANS * SPAN * 3 // 4, SPAN, 2))(jax.random.split(splits[10], DEVICES)).reshape((DEVICES, SPANS)).astype(jnp.int32),
    }


LEARN_RATE = 0.1
EPSILON = 1e-08

def complex_mul(left, right):
    middle = left.shape[-1] // 2
    left_real, left_imag = (left[..., :middle], left[..., middle:])
    right_real, right_imag = (right[..., :middle], right[..., middle:])
    return jnp.concatenate([left_real * right_real - left_imag * right_imag, left_real * right_imag + left_imag * right_real], -1)

def conj_mul(grad, other):
    middle = grad.shape[-1] // 2
    grad_real, grad_imag = (grad[..., :middle], grad[..., middle:])
    other_real, other_imag = (other[..., :middle], other[..., middle:])
    return jnp.concatenate([grad_real * other_real + grad_imag * other_imag, grad_imag * other_real - grad_real * other_imag], -1)

def span_terms(source, relation, target, negatives, weights):
    product = complex_mul(source, relation)
    product_b = product.astype(jnp.bfloat16)
    positive = lax.optimization_barrier(jnp.sum(product * target, -1))
    scores = lax.dot_general(product_b, negatives, (((1,), (1,)), ((), ())), preferred_element_type=jnp.float32)
    pos_grad = -jax.nn.sigmoid(-positive) * weights
    neg_grad = (jax.nn.sigmoid(scores) * weights[:, None]).astype(jnp.bfloat16)
    grad_product = pos_grad[:, None] * target + jnp.dot(neg_grad, negatives, preferred_element_type=jnp.float32)
    grad_target = pos_grad[:, None] * product
    grad_negatives = lax.dot_general(neg_grad, product_b, (((0,), (0,)), ((), ())), preferred_element_type=jnp.float32).astype(jnp.bfloat16)
    grad_source = conj_mul(grad_product, relation)
    grad_relation = conj_mul(grad_product, source)
    return (grad_source, grad_relation, grad_target, grad_negatives)

def row_adagrad(table, state, grad):
    new_state = state + lax.optimization_barrier(jnp.mean(grad * grad, -1))
    return (table - LEARN_RATE * grad / (jnp.sqrt(new_state)[:, None] + EPSILON), new_state)

def reference(left_table, right_table, left_state, right_state, relations, relation_state, source_rows, relation_ids, target_rows, negative_rows, span_sizes):
    positions = jnp.arange(SPAN, dtype=jnp.int32)
    owner_block = jnp.arange(NEG, dtype=jnp.int32) // NEG_PER

    def step(carry, index):
        grad_left, grad_right, grad_rel = carry
        device = index // SPANS
        group = device // N_SHARD
        source_ids = device * ROWS_DEV + source_rows[index]
        target_ids = device * ROWS_DEV + target_rows[index]
        negative_ids = (group * N_SHARD + owner_block) * ROWS_DEV + negative_rows[index]
        weights = (positions < span_sizes[device, index % SPANS]).astype(jnp.float32)
        source = left_table[source_ids]
        relation = relations[relation_ids[index]]
        target = right_table[target_ids]
        negatives = right_table[negative_ids].astype(jnp.bfloat16)
        grad_source, grad_relation, grad_target, grad_negatives = span_terms(source, relation, target, negatives, weights)
        grad_left = grad_left.at[source_ids].add(grad_source)
        grad_right = grad_right.at[target_ids].add(grad_target)
        grad_right = grad_right.at[negative_ids].add(grad_negatives.astype(jnp.float32))
        grad_rel = grad_rel.at[relation_ids[index]].add(grad_relation)
        return ((grad_left, grad_right, grad_rel), None)
    start = (jnp.zeros(left_table.shape, jnp.float32), jnp.zeros(right_table.shape, jnp.float32), jnp.zeros(relations.shape, jnp.float32))
    totals, unused = lax.scan(step, start, jnp.arange(source_rows.shape[0], dtype=jnp.int32))
    grad_left, grad_right, grad_rel = totals
    new_left, new_left_state = row_adagrad(left_table, left_state, grad_left)
    new_right, new_right_state = row_adagrad(right_table, right_state, grad_right)
    new_relations, new_relation_state = row_adagrad(relations, relation_state, grad_rel)
    order = jnp.mod(jnp.arange(N_GRP, dtype=jnp.int32) - ROUND, N_GRP)

    def regroup(array):
        blocks = array.reshape((N_GRP, -1) + array.shape[1:])
        return blocks[order].reshape(array.shape)
    return (regroup(new_left), regroup(new_left_state), regroup(new_right), regroup(new_right_state), new_relations, new_relation_state)
```

```python
import functools

import jax
import jax.numpy as jnp
from jax import lax
from jax.experimental import pallas as pl
from jax.experimental.pallas import tpu as pltpu
from jax.sharding import PartitionSpec as P

ROUND = 5
LEARN_RATE = 0.1
EPSILON = 1e-08

WIDTH = 400
HALF = 200
REST = HALF - 128
SPANS = 9
PEERS = 8
NEG_PER = 125
SLOT = 128
SPAN_PAD = 1024
ROWS = 4096
DUMP = ROWS
TALL = 4 * (ROWS + 8)
RELS = 1345
RELS_PAD = 1408
CORES = 2
CHIPS = 8
REL_SHARE = 48
REL_TALL = CORES * PEERS * CHIPS * REL_SHARE
PARTS = 1
PART = SPANS // PARTS
TILE = 256
SUB = 32
UNROLL = 16
CHUNKS = ((0, 128), (128, 200), (200, 328), (328, 400))
WIRE = 400

F32 = jnp.float32
BF16 = jnp.bfloat16
PARAMS = dict(vmem_limit_bytes=58 * 1024 * 1024)


def lane_ids(shape):
    return lax.broadcasted_iota(jnp.int32, shape, len(shape) - 1)


def to_rows(t_ref, out_ref, count):
    def block(i, _):
        at = pl.ds(pl.multiple_of(i * 128, 128), 128)
        for c, (low, high) in enumerate(CHUNKS):
            part = t_ref[low:high, at]
            if high - low < 128:
                part = jnp.concatenate([part, jnp.zeros((128 - (high - low), 128), F32)], 0)
            out_ref[pl.ds(i * 512 + c, 128, stride=4), :] = part.T
        return 0

    lax.fori_loop(0, count // 128, block, 0)


def adagrad_block(g_ref, t, state, i):
    parts = []
    for c, (low, high) in enumerate(CHUNKS):
        part = g_ref[pl.ds(i * 512 + c, 128, stride=4), :].T
        parts.append(part[: high - low])
    grad = jnp.concatenate(parts, 0)
    new_state = state + jnp.sum(grad * grad, 0, keepdims=True) * (1.0 / WIDTH)
    rate = LEARN_RATE / (jnp.sqrt(new_state) + EPSILON)
    return t - grad * rate, new_state


def adagrad_tables(g_ref, t_ref, state_ref, new_ref, new_state_ref):
    def block(i, _):
        at = pl.ds(pl.multiple_of(i * 128, 128), 128)
        new, state = adagrad_block(g_ref, t_ref[:, at], state_ref[:, at], i)
        new_ref[:, at] = new.astype(new_ref.dtype)
        new_state_ref[:, at] = state
        return 0

    lax.fori_loop(0, ROWS // 128, block, 0)


def spot(group, j):
    return pl.ds(group * (4 * UNROLL) + (j // 8) * 32 + (j % 8), 4, stride=8)


def row(index):
    return pl.ds(pl.multiple_of(index * 4, 4), 4)


def serve_kernel(ids, t_ref, out_ref, table, stage):
    peer = pl.program_id(0)

    @pl.when(peer == 0)
    def _():
        to_rows(t_ref, table, ROWS)
        table[4 * ROWS :, :] = jnp.zeros((TALL - 4 * ROWS, 128), F32)

    lanes = lane_ids((SLOT, 128))

    def span(c, _):
        base = peer * (SPANS * SLOT) + c * SLOT

        def group(g, _):
            for j in range(UNROLL):
                stage[spot(g, j), :] = table[row(ids[base + g * UNROLL + j]), :]
            return 0

        lax.fori_loop(0, SLOT // UNROLL, group, 0)
        s = stage[...].reshape(SLOT // 8, 4, 8, 128)
        re0, re1, im0, im1 = (s[:, k].reshape(SLOT, 128) for k in range(4))
        moved = pltpu.roll(im1, REST, 1)
        mixed = jnp.where(lanes < REST, re1, moved)
        tail = jnp.where(lanes < 16, moved, 0.0)
        packed = tail[:16]
        for k in range(1, 8):
            packed = packed + pltpu.roll(tail[16 * k : 16 * k + 16], 16 * k, 1)
        at = pl.multiple_of(c * WIRE, 16)
        out_ref[0, pl.ds(at, 128), :] = re0.astype(BF16)
        out_ref[0, pl.ds(at + 128, 128), :] = im0.astype(BF16)
        out_ref[0, pl.ds(at + 256, 128), :] = mixed.astype(BF16)
        out_ref[0, pl.ds(at + 384, 16), :] = packed.astype(BF16)
        return 0

    lax.fori_loop(0, SPANS, span, 0)


def serve(ids, table_t):
    return pl.pallas_call(
        serve_kernel,
        grid=(PEERS,),
        out_shape=jax.ShapeDtypeStruct((PEERS, SPANS * WIRE, 128), BF16),
        in_specs=[
            pl.BlockSpec(memory_space=pltpu.SMEM),
            pl.BlockSpec(memory_space=pltpu.VMEM),
        ],
        out_specs=pl.BlockSpec((1, SPANS * WIRE, 128), lambda p: (p, 0, 0)),
        scratch_shapes=[
            pltpu.VMEM((TALL, 128), F32),
            pltpu.VMEM((4 * SLOT, 128), F32),
        ],
        compiler_params=pltpu.CompilerParams(**PARAMS),
        cost_estimate=pl.CostEstimate(flops=0, bytes_accessed=80_000_000, transcendentals=0),
        name="serve",
    )(ids, table_t)


def unpack_wire(block):
    lanes = lane_ids((SLOT, 128))
    re0, im0, mixed, packed = block[:128], block[128:256], block[256:384], block[384:400]
    re1 = jnp.where(lanes < REST, mixed, 0.0)
    tail = jnp.concatenate([pltpu.roll(packed, (56 - 16 * k) % 128, 1) for k in range(8)], 0)
    im1 = jnp.where(lanes < 56, pltpu.roll(mixed, 56, 1), jnp.where(lanes < REST, tail, 0.0))
    return re0, re1, im0, im1


def forward_kernel(
    src, rel, tgt, live_ref, left_t, right_t, rel_t,
    s_out, b_out, p_out, pt_out, g_ref,
    left, right, rels, s_st, b_st, t_st, g_st,
):
    c = pl.program_id(0)

    @pl.when(c == 0)
    def _():
        to_rows(left_t, left, ROWS)
        to_rows(right_t, right, ROWS)
        to_rows(rel_t, rels, RELS_PAD)
        g_ref[...] = jnp.zeros_like(g_ref)
        for st in (s_st, b_st, t_st):
            st[...] = jnp.zeros_like(st)

    live = live_ref[c]

    def tile(t, _):
        base = c * SPAN_PAD + t * TILE
        left_over = jnp.minimum(live - t * TILE, TILE)
        groups = (left_over + UNROLL - 1) // UNROLL

        def gather(g, _):
            for j in range(UNROLL):
                e = base + g * UNROLL + j
                s_st[spot(g, j), :] = left[row(src[e]), :]
                b_st[spot(g, j), :] = rels[row(rel[e]), :]
                t_st[spot(g, j), :] = right[row(tgt[e]), :]
            return 0

        lax.fori_loop(0, groups, gather, 0)

        def sub(k, _):
            at = pl.ds(pl.multiple_of(k * (4 * SUB), 4 * SUB), 4 * SUB)
            s, b, q = (st[at, :].reshape(SUB // 8, 4, 8, 128) for st in (s_st, b_st, t_st))
            re = [s[:, i] * b[:, i] - s[:, i + 2] * b[:, i + 2] for i in range(2)]
            im = [s[:, i] * b[:, i + 2] + s[:, i + 2] * b[:, i] for i in range(2)]
            prod = re + im
            positive = jnp.sum(
                prod[0] * q[:, 0] + prod[1] * q[:, 1] + prod[2] * q[:, 2] + prod[3] * q[:, 3],
                -1, keepdims=True,
            )
            shape = (SUB // 8, 8, 1)
            where = (
                k * SUB
                + lax.broadcasted_iota(jnp.int32, shape, 0) * 8
                + lax.broadcasted_iota(jnp.int32, shape, 1)
            )
            pos_grad = jnp.where(where < left_over, -jax.nn.sigmoid(-positive), 0.0)
            g_st[at, :] = jnp.stack([pos_grad * x for x in prod], 1).reshape(4 * SUB, 128)
            rows = pl.ds(pl.multiple_of(t * TILE + k * SUB, SUB), SUB)
            for i in range(4):
                lanes = slice(i * 128, i * 128 + 128)
                s_out[0, rows, lanes] = s[:, i].reshape(SUB, 128).astype(BF16)
                b_out[0, rows, lanes] = b[:, i].reshape(SUB, 128).astype(BF16)
                p_out[0, rows, lanes] = prod[i].reshape(SUB, 128).astype(BF16)
                pt_out[0, rows, lanes] = (pos_grad * q[:, i]).reshape(SUB, 128).astype(BF16)
            return 0

        lax.fori_loop(0, TILE // SUB, sub, 0)

        def scatter(g, _):
            for j in range(UNROLL):
                at = row(tgt[base + g * UNROLL + j])
                g_ref[at, :] = g_ref[at, :] + g_st[spot(g, j), :]
            return 0

        lax.fori_loop(0, groups, scatter, 0)
        return 0

    lax.fori_loop(0, (live + TILE - 1) // TILE, tile, 0)


def forward(src, rel, tgt, live, left_t, right_t, rel_t):
    smem = pl.BlockSpec(memory_space=pltpu.SMEM)
    vmem = pl.BlockSpec(memory_space=pltpu.VMEM)
    per_edge = jax.ShapeDtypeStruct((SPANS, SPAN_PAD, 512), BF16)
    block = pl.BlockSpec((1, SPAN_PAD, 512), lambda c: (c, 0, 0))
    stage = pltpu.VMEM((4 * TILE, 128), F32)
    return pl.pallas_call(
        forward_kernel,
        grid=(SPANS,),
        out_shape=[per_edge] * 4 + [jax.ShapeDtypeStruct((4 * ROWS, 128), F32)],
        in_specs=[smem] * 4 + [vmem] * 3,
        out_specs=[block] * 4 + [vmem],
        scratch_shapes=[
            pltpu.VMEM((4 * ROWS, 128), F32),
            pltpu.VMEM((4 * ROWS, 128), F32),
            pltpu.VMEM((4 * RELS_PAD, 128), F32),
        ]
        + [stage] * 4,
        compiler_params=pltpu.CompilerParams(**PARAMS),
        cost_estimate=pl.CostEstimate(flops=0, bytes_accessed=280_000_000, transcendentals=0),
        name="forward",
    )(src, rel, tgt, live, left_t, right_t, rel_t)


def negatives_kernel(first, live_ref, p_ref, pt_ref, got_ref, *rest):
    gp_ref, back_ref, neg, acc = rest[-4:]
    c = pl.program_id(0)
    live = live_ref[first + c]

    def unpack(p, _):
        block = got_ref[p].astype(F32)
        at = pl.ds(pl.multiple_of(p * SLOT, SLOT), SLOT)
        for k, part in enumerate(unpack_wire(block)):
            neg[at, k * 128 : k * 128 + 128] = part.astype(BF16)
        return 0

    lax.fori_loop(0, PEERS, unpack, 0)
    acc[...] = jnp.zeros_like(acc)

    def tile(t, _):
        rows = pl.ds(pl.multiple_of(t * TILE, TILE), TILE)
        product = p_ref[0, rows, :]
        scores = lax.dot_general(
            product, neg[...], (((1,), (1,)), ((), ())), preferred_element_type=F32
        )
        where = t * TILE + lax.broadcasted_iota(jnp.int32, (TILE, 1), 0)
        weight = (where < live).astype(F32) * 0.5
        grad = (weight * jnp.tanh(scores * 0.5) + weight).astype(BF16)
        gp = jnp.dot(grad, neg[...], preferred_element_type=F32)
        gp_ref[0, rows, :] = (gp + pt_ref[0, rows, :].astype(F32)).astype(BF16)
        acc[...] += lax.dot_general(
            grad, product, (((0,), (0,)), ((), ())), preferred_element_type=F32
        )
        return 0

    lax.fori_loop(0, (live + TILE - 1) // TILE, tile, 0)

    lanes = lane_ids((SLOT, 128))

    def pack(p, _):
        g = acc[pl.ds(pl.multiple_of(p * SLOT, SLOT), SLOT), :]
        re0, re1, im0, im1 = (g[:, k * 128 : k * 128 + 128] for k in range(4))
        moved = pltpu.roll(im1, REST, 1)
        tail = jnp.where(lanes < 16, moved, 0.0)
        packed = tail[:16]
        for k in range(1, 8):
            packed = packed + pltpu.roll(tail[16 * k : 16 * k + 16], 16 * k, 1)
        back_ref[p, 0:128, :] = re0.astype(BF16)
        back_ref[p, 128:256, :] = im0.astype(BF16)
        back_ref[p, 256:384, :] = jnp.where(lanes < REST, re1, moved).astype(BF16)
        back_ref[p, 384:400, :] = packed.astype(BF16)
        return 0

    lax.fori_loop(0, PEERS, pack, 0)


def negatives(live, product, pos_target, got, first, grad_product):
    block = pl.BlockSpec((1, SPAN_PAD, 512), lambda c: (first + c, 0, 0))
    wire = pl.BlockSpec((PEERS, WIRE, 128), lambda c: (0, first + c, 0))
    operands = [live, product, pos_target, got]
    specs = [pl.BlockSpec(memory_space=pltpu.SMEM), block, block, wire]
    aliases = {}
    if grad_product is not None:
        operands.append(grad_product)
        specs.append(pl.BlockSpec(memory_space=pl.ANY))
        aliases = {4: 0}
    return pl.pallas_call(
        functools.partial(negatives_kernel, first),
        grid=(PART,),
        out_shape=[
            jax.ShapeDtypeStruct((SPANS, SPAN_PAD, 512), BF16),
            jax.ShapeDtypeStruct((PEERS, PART * WIRE, 128), BF16),
        ],
        in_specs=specs,
        out_specs=[block, pl.BlockSpec((PEERS, WIRE, 128), lambda c: (0, c, 0))],
        scratch_shapes=[
            pltpu.VMEM((PEERS * SLOT, 512), BF16),
            pltpu.VMEM((PEERS * SLOT, 512), F32),
        ],
        input_output_aliases=aliases,
        compiler_params=pltpu.CompilerParams(**PARAMS),
        cost_estimate=pl.CostEstimate(
            flops=14_000_000_000, bytes_accessed=60_000_000, transcendentals=3_000_000
        ),
        name="negatives",
    )(*operands)


def left_kernel(
    src, rel, live_ref, s_ref, b_ref, gp_ref, left_t, state, new_ref, new_state, rel_out, gleft, grel, a_st, r_st
):
    c = pl.program_id(0)

    @pl.when(c == 0)
    def _():
        gleft[...] = jnp.zeros_like(gleft)
        grel[...] = jnp.zeros_like(grel)

    live = live_ref[c]

    def tile(t, _):
        base = c * SPAN_PAD + t * TILE
        groups = (jnp.minimum(live - t * TILE, TILE) + UNROLL - 1) // UNROLL

        def sub(k, _):
            rows = pl.ds(pl.multiple_of(t * TILE + k * SUB, SUB), SUB)
            s, b, g = (
                [
                    ref[0, rows, i * 128 : i * 128 + 128].astype(F32).reshape(SUB // 8, 8, 128)
                    for i in range(4)
                ]
                for ref in (s_ref, b_ref, gp_ref)
            )
            at = pl.ds(pl.multiple_of(k * (4 * SUB), 4 * SUB), 4 * SUB)
            for st, o in ((a_st, b), (r_st, s)):
                re = [g[i] * o[i] + g[i + 2] * o[i + 2] for i in range(2)]
                im = [g[i + 2] * o[i] - g[i] * o[i + 2] for i in range(2)]
                st[at, :] = jnp.stack(re + im, 1).reshape(4 * SUB, 128)
            return 0

        lax.fori_loop(0, TILE // SUB, sub, 0)

        def scatter(g, _):
            for j in range(UNROLL):
                e = base + g * UNROLL + j
                at, to = row(src[e]), row(rel[e])
                gleft[at, :] = gleft[at, :] + a_st[spot(g, j), :]
                grel[to, :] = grel[to, :] + r_st[spot(g, j), :]
            return 0

        lax.fori_loop(0, groups, scatter, 0)
        return 0

    lax.fori_loop(0, (live + TILE - 1) // TILE, tile, 0)

    @pl.when(c == SPANS - 1)
    def _():
        rel_out[...] = grel[...].astype(BF16)
        adagrad_tables(gleft, left_t, state, new_ref, new_state)


def left_update(src, rel, live, source, relation, grad_product, left_t, state):
    smem = pl.BlockSpec(memory_space=pltpu.SMEM)
    vmem = pl.BlockSpec(memory_space=pltpu.VMEM)
    block = pl.BlockSpec((1, SPAN_PAD, 512), lambda c: (c, 0, 0))
    return pl.pallas_call(
        left_kernel,
        grid=(SPANS,),
        out_shape=[
            jax.ShapeDtypeStruct((WIDTH, ROWS), F32),
            jax.ShapeDtypeStruct((1, ROWS), F32),
            jax.ShapeDtypeStruct((REL_TALL, 128), BF16),
        ],
        in_specs=[smem] * 3 + [block] * 3 + [vmem] * 2,
        out_specs=[vmem] * 3,
        scratch_shapes=[pltpu.VMEM((4 * ROWS, 128), F32), pltpu.VMEM((REL_TALL, 128), F32)]
        + [pltpu.VMEM((4 * TILE, 128), F32)] * 2,
        compiler_params=pltpu.CompilerParams(**PARAMS),
        cost_estimate=pl.CostEstimate(flops=0, bytes_accessed=240_000_000, transcendentals=0),
        name="left_update",
    )(src, rel, live, source, relation, grad_product, left_t, state)


def right_kernel(ids, *refs):
    backs = refs[:PARTS]
    g_hbm, right_t, state, new_ref, new_state, total, stage, sem = refs[PARTS:]
    c = pl.program_id(0)

    @pl.when(c == 0)
    def _():
        copy = pltpu.make_async_copy(g_hbm, total.at[pl.ds(0, 4 * ROWS)], sem)
        copy.start()
        copy.wait()

    def peer(back_ref, p, _):
        parts = unpack_wire(back_ref[p].astype(F32))
        stage[...] = jnp.stack(
            [part.reshape(SLOT // 8, 8, 128) for part in parts], 1
        ).reshape(4 * SLOT, 128)
        base = p * (SPANS * SLOT) + c * SLOT

        def scatter(g, _):
            for j in range(UNROLL):
                at = row(ids[base + g * UNROLL + j])
                total[at, :] = total[at, :] + stage[spot(g, j), :]
            return 0

        lax.fori_loop(0, SLOT // UNROLL, scatter, 0)
        return 0

    for k, back_ref in enumerate(backs):

        @pl.when(c // PART == k)
        def _():
            lax.fori_loop(0, PEERS, functools.partial(peer, back_ref), 0)

    @pl.when(c == SPANS - 1)
    def _():
        adagrad_tables(total, right_t, state, new_ref, new_state)


def right_update(ids, backs, grad, right_t, state):
    def part(k):
        return pl.BlockSpec(
            (PEERS, WIRE, 128), lambda c: (0, jnp.clip(c - k * PART, 0, PART - 1), 0)
        )

    vmem = pl.BlockSpec(memory_space=pltpu.VMEM)
    return pl.pallas_call(
        right_kernel,
        grid=(SPANS,),
        out_shape=[
            jax.ShapeDtypeStruct((WIDTH, ROWS), F32),
            jax.ShapeDtypeStruct((1, ROWS), F32),
        ],
        in_specs=[
            pl.BlockSpec(memory_space=pltpu.SMEM),
            *(part(k) for k in range(PARTS)),
            pl.BlockSpec(memory_space=pl.ANY),
            vmem,
            vmem,
        ],
        out_specs=[vmem] * 2,
        scratch_shapes=[
            pltpu.VMEM((TALL, 128), F32),
            pltpu.VMEM((4 * SLOT, 128), F32),
            pltpu.SemaphoreType.DMA,
        ],
        compiler_params=pltpu.CompilerParams(**PARAMS),
        cost_estimate=pl.CostEstimate(flops=0, bytes_accessed=160_000_000, transcendentals=0),
        name="right_update",
    )(ids, *backs, grad, right_t, state)


def places():
    grp, shard = lax.axis_index("grp"), lax.axis_index("shard")
    core, chip = lax.rem(grp, CORES), lax.div(grp, CORES)

    def other_core():
        return (chip * CORES + 1 - core, shard)

    def along_grp(d):
        return (lax.rem(chip + d, CHIPS) * CORES + core, shard)

    def along_shard(d):
        return (grp, lax.rem(shard + d, PEERS))

    return core, chip, shard, other_core, along_grp, along_shard


def greet(devices):
    barrier = pltpu.get_barrier_semaphore()
    for device in devices:
        pl.semaphore_signal(
            barrier, inc=1, device_id=device, device_id_type=pl.DeviceIdType.MESH
        )
    pl.semaphore_wait(barrier, len(devices))


def sender(sends, recvs):
    def send(src, dst, slot, to):
        copy = pltpu.make_async_remote_copy(
            src_ref=src, dst_ref=dst, send_sem=sends.at[slot], recv_sem=recvs.at[slot],
            device_id=to, device_id_type=pl.DeviceIdType.MESH,
        )
        copy.start()
        return copy

    return send


def relation_sum_kernel(mine, out, got_0, half, got_1, sum_1, got_2, sum_2, sends, recvs):
    core, chip, shard, other_core, along_grp, along_shard = places()
    steps = range(1, PEERS)
    greet(
        [other_core()] + [along_shard(d) for d in steps] + [along_grp(d) for d in steps]
    )
    send = sender(sends, recvs)
    copy = send(mine.at[1 - core], got_0, 0, other_core())
    copy.wait()

    def add(p, _):
        half[p] = (mine[core, p].astype(F32) + got_0[p].astype(F32)).astype(BF16)
        return 0

    lax.fori_loop(0, PEERS, add, 0)
    copies = [
        send(half.at[lax.rem(shard + d, PEERS)], got_1.at[d - 1], d, along_shard(d))
        for d in steps
    ]
    for copy in copies:
        copy.wait()

    def total_of(k, _):
        total = mine[core, shard, k].astype(F32) + got_0[shard, k].astype(F32)
        for d in range(PEERS - 1):
            total = total + got_1[d, k].astype(F32)
        sum_1[k] = total
        return 0

    lax.fori_loop(0, CHIPS, total_of, 0)
    copies = [
        send(sum_1.at[lax.rem(chip + d, CHIPS)], got_2.at[d - 1], 7 + d, along_grp(d))
        for d in steps
    ]
    for copy in copies:
        copy.wait()
    total = sum_1[chip]
    for d in range(CHIPS - 1):
        total = total + got_2[d]
    sum_2[...] = total
    out[chip] = total
    copies = [send(sum_2, out.at[chip], 14 + d, along_grp(d)) for d in steps]
    for copy in copies:
        copy.wait()


def relation_sum(grad):
    vmem = pl.BlockSpec(memory_space=pltpu.VMEM)
    return pl.pallas_call(
        relation_sum_kernel,
        out_shape=jax.ShapeDtypeStruct((CHIPS, REL_SHARE, 128), F32),
        in_specs=[vmem],
        out_specs=vmem,
        scratch_shapes=[
            pltpu.VMEM((PEERS, CHIPS, REL_SHARE, 128), BF16),
            pltpu.VMEM((PEERS, CHIPS, REL_SHARE, 128), BF16),
            pltpu.VMEM((PEERS - 1, CHIPS, REL_SHARE, 128), BF16),
            pltpu.VMEM((CHIPS, REL_SHARE, 128), F32),
            pltpu.VMEM((CHIPS - 1, REL_SHARE, 128), F32),
            pltpu.VMEM((REL_SHARE, 128), F32),
            pltpu.SemaphoreType.DMA((22,)),
            pltpu.SemaphoreType.DMA((22,)),
        ],
        compiler_params=pltpu.CompilerParams(
            collective_id=0, has_side_effects=True, vmem_limit_bytes=32 * 1024 * 1024
        ),
        cost_estimate=pl.CostEstimate(flops=0, bytes_accessed=4_000_000, transcendentals=0),
        name="relation_sum",
    )(grad.reshape(CORES, PEERS, CHIPS, REL_SHARE, 128))


def relation_spread_kernel(mine, out, sends, recvs):
    core, chip, shard, other_core, along_grp, along_shard = places()
    steps = range(1, PEERS)
    greet([other_core()] + [along_shard(d) for d in steps])
    send = sender(sends, recvs)
    copies = [send(mine, out.at[core, shard], d, along_shard(d)) for d in steps]
    out[core, shard] = mine[...]
    across = [send(mine, out.at[core, shard], 8, other_core())]
    for d in steps:
        copies[d - 1].wait_recv()
        block = out.at[core, lax.rem(shard + PEERS - d, PEERS)]
        across.append(send(block, block, 8 + d, other_core()))
    for copy in copies:
        copy.wait_send()
    for copy in across:
        copy.wait()


def relation_spread(total):
    vmem = pl.BlockSpec(memory_space=pltpu.VMEM)
    out = pl.pallas_call(
        relation_spread_kernel,
        out_shape=jax.ShapeDtypeStruct((CORES, PEERS, CHIPS, REL_SHARE, 128), F32),
        in_specs=[vmem],
        out_specs=vmem,
        scratch_shapes=[pltpu.SemaphoreType.DMA((16,)), pltpu.SemaphoreType.DMA((16,))],
        compiler_params=pltpu.CompilerParams(
            collective_id=1, has_side_effects=True, vmem_limit_bytes=32 * 1024 * 1024
        ),
        cost_estimate=pl.CostEstimate(flops=0, bytes_accessed=4_000_000, transcendentals=0),
        name="relation_spread",
    )(total)
    return out.reshape(REL_TALL, 128)


def relation_kernel(g_ref, rel_t, state, new_ref, new_state):
    for i in range(RELS_PAD // 128):
        low, high = i * 128, min(RELS, i * 128 + 128)
        new, ns = adagrad_block(g_ref, rel_t[:, low : low + 128], state[:, low : low + 128], i)
        new_ref[:, low:high] = new[:, : high - low]
        new_state[:, low:high] = ns[:, : high - low]


def relation_update(grad, rel_t, state):
    vmem = pl.BlockSpec(memory_space=pltpu.VMEM)
    return pl.pallas_call(
        relation_kernel,
        out_shape=[
            jax.ShapeDtypeStruct((WIDTH, RELS), F32),
            jax.ShapeDtypeStruct((1, RELS), F32),
        ],
        in_specs=[vmem] * 3,
        out_specs=[vmem] * 2,
        compiler_params=pltpu.CompilerParams(**PARAMS),
        name="relation_update",
    )(grad, rel_t, state)


def passed_along(block, axis, distance):
    devices = range(lax.axis_size(axis))
    route = [((i - distance) % len(devices), i) for i in devices]
    return lax.ppermute(block, axis, route)


def exchange(x):
    return lax.all_to_all(x, "shard", split_axis=0, concat_axis=0, tiled=True)


def local(
    left_table, right_table, left_state, right_state, relations, relation_state,
    source_rows, relation_ids, target_rows, negative_rows, span_sizes,
):
    left_t, right_t = left_table.T, right_table.T
    wanted = negative_rows.reshape(SPANS, PEERS, NEG_PER).transpose(1, 0, 2)
    wanted = jnp.pad(wanted, ((0, 0), (0, 0), (0, SLOT - NEG_PER)), constant_values=DUMP)
    asked = exchange(wanted.reshape(PEERS, SPANS * SLOT)).reshape(-1)
    served = serve(asked, right_t)
    got = exchange(served)

    def flat(ids):
        return jnp.pad(ids, ((0, 0), (0, SPAN_PAD - ids.shape[1]))).reshape(-1)

    src, rel, tgt = flat(source_rows), flat(relation_ids), flat(target_rows)
    live = span_sizes.reshape(SPANS)
    rel_t = jnp.pad(relations.T, ((0, 0), (0, RELS_PAD - RELS)))
    rel_state = jnp.pad(relation_state, (0, RELS_PAD - RELS), constant_values=1.0)
    source, relation, product, pos_target, grad_right = forward(
        src, rel, tgt, live, left_t, right_t, rel_t
    )
    grad_product, returned = None, []
    for k in range(PARTS):
        grad_product, back = negatives(live, product, pos_target, got, k * PART, grad_product)
        returned.append(exchange(back))
    new_left, new_left_state, grad_rel = left_update(
        src, rel, live, source, relation, grad_product, left_t, left_state.reshape(1, ROWS)
    )
    rel_share = relation_sum(grad_rel)
    sent_left, returned, rel_share = lax.optimization_barrier(
        (new_left.astype(jnp.float16), returned, rel_share)
    )
    moved_left = passed_along(sent_left, "grp", ROUND)
    new_right, new_right_state = right_update(
        asked, returned, grad_right, right_t, right_state.reshape(1, ROWS)
    )
    rel_share, sent = lax.optimization_barrier((rel_share, new_right.astype(jnp.float16)))
    rel_total = relation_spread(rel_share)
    moved_right = passed_along(sent, "grp", ROUND)
    states = jnp.concatenate([new_left_state, new_right_state], 0)
    moved_states = passed_along(states, "grp", ROUND)
    new_rel, new_rel_state = relation_update(rel_total, rel_t, rel_state.reshape(1, RELS_PAD))
    new_rel, moved_left, moved_states = lax.optimization_barrier(
        (new_rel, moved_left, moved_states)
    )
    return (
        moved_left.astype(F32).T,
        moved_states[0],
        moved_right.astype(F32).T,
        moved_states[1],
        new_rel.T,
        new_rel_state.reshape(RELS),
    )


def solution(mesh):
    rows, flat = P(("grp", "shard"), None), P(("grp", "shard"))
    return jax.shard_map(
        local,
        mesh=mesh,
        in_specs=(rows, rows, flat, flat, P(), P(), rows, rows, rows, rows, rows),
        out_specs=(rows, flat, rows, flat, P(), P()),
        check_vma=False,
    )
```

```python
import functools

import jax
import jax.numpy as jnp
from jax import lax
from jax.experimental import pallas as pl
from jax.experimental.pallas import tpu as pltpu
from jax.sharding import PartitionSpec as P

ROUND = 5
LEARN_RATE = 0.1
EPSILON = 1e-08

WIDTH = 400
HALF = 200
REST = HALF - 128
SPANS = 9
PEERS = 8
NEG_PER = 125
SLOT = 128
SPAN_PAD = 1024
ROWS = 4096
DUMP = ROWS
TALL = 4 * (ROWS + 8)
RELS = 1345
RELS_PAD = 1408
CORES = 2
CHIPS = 8
REL_SHARE = 48
REL_TALL = CORES * PEERS * CHIPS * REL_SHARE
PARTS = 1
PART = SPANS // PARTS
TILE = 256
SUB = 32
UNROLL = 16
CHUNKS = ((0, 128), (128, 200), (200, 328), (328, 400))
WIRE = 400

F32 = jnp.float32
BF16 = jnp.bfloat16
PARAMS = dict(vmem_limit_bytes=58 * 1024 * 1024)


def lane_ids(shape):
    return lax.broadcasted_iota(jnp.int32, shape, len(shape) - 1)


def to_rows(t_ref, out_ref, count):
    def block(i, _):
        at = pl.ds(pl.multiple_of(i * 128, 128), 128)
        for c, (low, high) in enumerate(CHUNKS):
            part = t_ref[low:high, at]
            if high - low < 128:
                part = jnp.concatenate([part, jnp.zeros((128 - (high - low), 128), F32)], 0)
            out_ref[pl.ds(i * 512 + c, 128, stride=4), :] = part.T
        return 0

    lax.fori_loop(0, count // 128, block, 0, unroll=8 if count == ROWS else 1)


def adagrad_block(g_ref, t, state, i):
    parts = []
    for c, (low, high) in enumerate(CHUNKS):
        part = g_ref[pl.ds(i * 512 + c, 128, stride=4), :].T
        parts.append(part[: high - low])
    grad = jnp.concatenate(parts, 0)
    new_state = state + jnp.sum(grad * grad, 0, keepdims=True) * (1.0 / WIDTH)
    rate = LEARN_RATE / (jnp.sqrt(new_state) + EPSILON)
    return t - grad * rate, new_state


def adagrad_tables(g_ref, t_ref, state_ref, new_ref, new_state_ref):
    def block(i, _):
        at = pl.ds(pl.multiple_of(i * 128, 128), 128)
        new, state = adagrad_block(g_ref, t_ref[:, at], state_ref[:, at], i)
        new_ref[:, at] = new.astype(new_ref.dtype)
        new_state_ref[:, at] = state
        return 0

    lax.fori_loop(0, ROWS // 128, block, 0, unroll=2)


def spot(group, j):
    return pl.ds(group * (4 * UNROLL) + 4 * j, 4)


def chunk(first, count, c):
    return pl.ds(first * 4 + c, count, stride=4)


def row(index):
    return pl.ds(pl.multiple_of(index * 4, 4), 4)


TOGETHER = 1


def add_rows(*work):
    for first in range(0, len(work[0][1]), TOGETHER):
        for ref, indices, values in work:
            ids = indices[first : first + TOGETHER]
            adds = [value() for value in values[first : first + TOGETHER]]
            new = [ref[row(i), :] + add for i, add in zip(ids, adds)]
            for k in range(len(ids)):
                for j in range(k):
                    same = jnp.where(ids[j] == ids[k], 1.0, 0.0)
                    new[k] = new[k] + same * adds[j]
            for i, value in zip(ids, new):
                ref[row(i), :] = value


def staged(stage, group):
    return [functools.partial(lambda j: stage[spot(group, j), :], j) for j in range(UNROLL)]


def serve_kernel(ids, t_ref, out_ref, table, stage):
    peer = pl.program_id(0)

    @pl.when(peer == 0)
    def _():
        to_rows(t_ref, table, ROWS)
        table[4 * ROWS :, :] = jnp.zeros((TALL - 4 * ROWS, 128), F32)

    lanes = lane_ids((SLOT, 128))

    def span(c, _):
        base = peer * (SPANS * SLOT) + c * SLOT

        def group(g, _):
            for j in range(UNROLL):
                stage[spot(g, j), :] = table[row(ids[base + g * UNROLL + j]), :]
            return 0

        lax.fori_loop(0, SLOT // UNROLL, group, 0, unroll=8)
        re0, re1, im0, im1 = (stage[chunk(0, SLOT, k), :] for k in range(4))
        moved = pltpu.roll(im1, REST, 1)
        mixed = jnp.where(lanes < REST, re1, moved)
        tail = jnp.where(lanes < 16, moved, 0.0)
        packed = tail[:16]
        for k in range(1, 8):
            packed = packed + pltpu.roll(tail[16 * k : 16 * k + 16], 16 * k, 1)
        at = pl.multiple_of(c * WIRE, 16)
        out_ref[0, pl.ds(at, 128), :] = re0.astype(BF16)
        out_ref[0, pl.ds(at + 128, 128), :] = im0.astype(BF16)
        out_ref[0, pl.ds(at + 256, 128), :] = mixed.astype(BF16)
        out_ref[0, pl.ds(at + 384, 16), :] = packed.astype(BF16)
        return 0

    lax.fori_loop(0, SPANS, span, 0)


def serve(ids, table_t):
    return pl.pallas_call(
        serve_kernel,
        grid=(PEERS,),
        out_shape=jax.ShapeDtypeStruct((PEERS, SPANS * WIRE, 128), BF16),
        in_specs=[
            pl.BlockSpec(memory_space=pltpu.SMEM),
            pl.BlockSpec(memory_space=pltpu.VMEM),
        ],
        out_specs=pl.BlockSpec((1, SPANS * WIRE, 128), lambda p: (p, 0, 0)),
        scratch_shapes=[
            pltpu.VMEM((TALL, 128), F32),
            pltpu.VMEM((4 * SLOT, 128), F32),
        ],
        compiler_params=pltpu.CompilerParams(**PARAMS),
        cost_estimate=pl.CostEstimate(flops=0, bytes_accessed=80_000_000, transcendentals=0),
        name="serve",
    )(ids, table_t)


def unpack_wire(block):
    lanes = lane_ids((SLOT, 128))
    re0, im0, mixed, packed = block[:128], block[128:256], block[256:384], block[384:400]
    re1 = jnp.where(lanes < REST, mixed, 0.0)
    tail = jnp.concatenate([pltpu.roll(packed, (56 - 16 * k) % 128, 1) for k in range(8)], 0)
    im1 = jnp.where(lanes < 56, pltpu.roll(mixed, 56, 1), jnp.where(lanes < REST, tail, 0.0))
    return re0, re1, im0, im1


def forward_kernel(
    src, rel, tgt, live_ref, left_t, right_t, rel_t,
    s_out, b_out, p_out, pt_out, g_ref,
    left, right, rels, s_st, b_st, t_st, g_st,
):
    c = pl.program_id(0)

    @pl.when(c == 0)
    def _():
        to_rows(left_t, left, ROWS)
        to_rows(right_t, right, ROWS)
        to_rows(rel_t, rels, RELS_PAD)
        g_ref[...] = jnp.zeros_like(g_ref)
        for st in (s_st, b_st, t_st):
            st[...] = jnp.zeros_like(st)

    live = live_ref[c]

    def tile(t, _):
        base = c * SPAN_PAD + t * TILE
        left_over = jnp.minimum(live - t * TILE, TILE)
        groups = (left_over + UNROLL - 1) // UNROLL

        def gather(g, _):
            for j in range(UNROLL):
                e = base + g * UNROLL + j
                s_st[spot(g, j), :] = left[row(src[e]), :]
                b_st[spot(g, j), :] = rels[row(rel[e]), :]
                t_st[spot(g, j), :] = right[row(tgt[e]), :]
            return 0

        lax.fori_loop(0, groups, gather, 0)

        def sub(k, _):
            s, b, q = (
                [st[chunk(k * SUB, SUB, i), :] for i in range(4)] for st in (s_st, b_st, t_st)
            )
            re = [s[i] * b[i] - s[i + 2] * b[i + 2] for i in range(2)]
            im = [s[i] * b[i + 2] + s[i + 2] * b[i] for i in range(2)]
            prod = re + im
            positive = jnp.sum(
                prod[0] * q[0] + prod[1] * q[1] + prod[2] * q[2] + prod[3] * q[3],
                -1, keepdims=True,
            )
            where = k * SUB + lax.broadcasted_iota(jnp.int32, (SUB, 1), 0)
            pos_grad = jnp.where(where < left_over, -jax.nn.sigmoid(-positive), 0.0)
            for i in range(4):
                g_st[chunk(k * SUB, SUB, i), :] = pos_grad * prod[i]
            rows = pl.ds(pl.multiple_of(t * TILE + k * SUB, SUB), SUB)
            for i in range(4):
                lanes = slice(i * 128, i * 128 + 128)
                s_out[0, rows, lanes] = s[i].astype(BF16)
                b_out[0, rows, lanes] = b[i].astype(BF16)
                p_out[0, rows, lanes] = prod[i].astype(BF16)
                pt_out[0, rows, lanes] = (pos_grad * q[i]).astype(BF16)
            return 0

        lax.fori_loop(0, TILE // SUB, sub, 0, unroll=8)

        def scatter(g, _):
            ids = [tgt[base + g * UNROLL + j] for j in range(UNROLL)]
            add_rows((g_ref, ids, staged(g_st, g)))
            return 0

        lax.fori_loop(0, groups, scatter, 0)
        return 0

    lax.fori_loop(0, (live + TILE - 1) // TILE, tile, 0)


def forward(src, rel, tgt, live, left_t, right_t, rel_t):
    smem = pl.BlockSpec(memory_space=pltpu.SMEM)
    vmem = pl.BlockSpec(memory_space=pltpu.VMEM)
    per_edge = jax.ShapeDtypeStruct((SPANS, SPAN_PAD, 512), BF16)
    block = pl.BlockSpec((1, SPAN_PAD, 512), lambda c: (c, 0, 0))
    stage = pltpu.VMEM((4 * TILE, 128), F32)
    return pl.pallas_call(
        forward_kernel,
        grid=(SPANS,),
        out_shape=[per_edge] * 4 + [jax.ShapeDtypeStruct((4 * ROWS, 128), F32)],
        in_specs=[smem] * 4 + [vmem] * 3,
        out_specs=[block] * 4 + [vmem],
        scratch_shapes=[
            pltpu.VMEM((4 * ROWS, 128), F32),
            pltpu.VMEM((4 * ROWS, 128), F32),
            pltpu.VMEM((4 * RELS_PAD, 128), F32),
        ]
        + [stage] * 4,
        compiler_params=pltpu.CompilerParams(**PARAMS),
        cost_estimate=pl.CostEstimate(flops=0, bytes_accessed=280_000_000, transcendentals=0),
        name="forward",
    )(src, rel, tgt, live, left_t, right_t, rel_t)


def negatives_kernel(first, live_ref, p_ref, pt_ref, got_ref, *rest):
    gp_ref, back_ref, neg, acc = rest[-4:]
    c = pl.program_id(0)
    live = live_ref[first + c]

    def unpack(p, _):
        block = got_ref[p].astype(F32)
        at = pl.ds(pl.multiple_of(p * SLOT, SLOT), SLOT)
        for k, part in enumerate(unpack_wire(block)):
            neg[at, k * 128 : k * 128 + 128] = part.astype(BF16)
        return 0

    lax.fori_loop(0, PEERS, unpack, 0, unroll=4)
    acc[...] = jnp.zeros_like(acc)

    def tile(t, _):
        rows = pl.ds(pl.multiple_of(t * TILE, TILE), TILE)
        product = p_ref[0, rows, :]
        scores = lax.dot_general(
            product, neg[...], (((1,), (1,)), ((), ())), preferred_element_type=F32
        )
        where = t * TILE + lax.broadcasted_iota(jnp.int32, (TILE, 1), 0)
        weight = (where < live).astype(F32) * 0.5
        grad = (weight * jnp.tanh(scores * 0.5) + weight).astype(BF16)
        gp = jnp.dot(grad, neg[...], preferred_element_type=F32)
        gp_ref[0, rows, :] = (gp + pt_ref[0, rows, :].astype(F32)).astype(BF16)
        acc[...] += lax.dot_general(
            grad, product, (((0,), (0,)), ((), ())), preferred_element_type=F32
        )
        return 0

    lax.fori_loop(0, (live + TILE - 1) // TILE, tile, 0)

    lanes = lane_ids((SLOT, 128))

    def pack(p, _):
        g = acc[pl.ds(pl.multiple_of(p * SLOT, SLOT), SLOT), :]
        re0, re1, im0, im1 = (g[:, k * 128 : k * 128 + 128] for k in range(4))
        moved = pltpu.roll(im1, REST, 1)
        tail = jnp.where(lanes < 16, moved, 0.0)
        packed = tail[:16]
        for k in range(1, 8):
            packed = packed + pltpu.roll(tail[16 * k : 16 * k + 16], 16 * k, 1)
        back_ref[p, 0:128, :] = re0.astype(BF16)
        back_ref[p, 128:256, :] = im0.astype(BF16)
        back_ref[p, 256:384, :] = jnp.where(lanes < REST, re1, moved).astype(BF16)
        back_ref[p, 384:400, :] = packed.astype(BF16)
        return 0

    lax.fori_loop(0, PEERS, pack, 0, unroll=4)


def negatives(live, product, pos_target, got, first, grad_product):
    block = pl.BlockSpec((1, SPAN_PAD, 512), lambda c: (first + c, 0, 0))
    wire = pl.BlockSpec((PEERS, WIRE, 128), lambda c: (0, first + c, 0))
    operands = [live, product, pos_target, got]
    specs = [pl.BlockSpec(memory_space=pltpu.SMEM), block, block, wire]
    aliases = {}
    if grad_product is not None:
        operands.append(grad_product)
        specs.append(pl.BlockSpec(memory_space=pl.ANY))
        aliases = {4: 0}
    return pl.pallas_call(
        functools.partial(negatives_kernel, first),
        grid=(PART,),
        out_shape=[
            jax.ShapeDtypeStruct((SPANS, SPAN_PAD, 512), BF16),
            jax.ShapeDtypeStruct((PEERS, PART * WIRE, 128), BF16),
        ],
        in_specs=specs,
        out_specs=[block, pl.BlockSpec((PEERS, WIRE, 128), lambda c: (0, c, 0))],
        scratch_shapes=[
            pltpu.VMEM((PEERS * SLOT, 512), BF16),
            pltpu.VMEM((PEERS * SLOT, 512), F32),
        ],
        input_output_aliases=aliases,
        compiler_params=pltpu.CompilerParams(**PARAMS),
        cost_estimate=pl.CostEstimate(
            flops=14_000_000_000, bytes_accessed=60_000_000, transcendentals=3_000_000
        ),
        name="negatives",
    )(*operands)


def left_kernel(
    src, rel, live_ref, s_ref, b_ref, gp_ref, left_t, state, new_ref, new_state, rel_out, gleft, grel, a_st, r_st
):
    c = pl.program_id(0)

    @pl.when(c == 0)
    def _():
        gleft[...] = jnp.zeros_like(gleft)
        grel[...] = jnp.zeros_like(grel)

    live = live_ref[c]

    def tile(t, _):
        base = c * SPAN_PAD + t * TILE
        groups = (jnp.minimum(live - t * TILE, TILE) + UNROLL - 1) // UNROLL

        def sub(k, _):
            rows = pl.ds(pl.multiple_of(t * TILE + k * SUB, SUB), SUB)
            s, b, g = (
                [ref[0, rows, i * 128 : i * 128 + 128].astype(F32) for i in range(4)]
                for ref in (s_ref, b_ref, gp_ref)
            )
            for st, o in ((a_st, b), (r_st, s)):
                re = [g[i] * o[i] + g[i + 2] * o[i + 2] for i in range(2)]
                im = [g[i + 2] * o[i] - g[i] * o[i + 2] for i in range(2)]
                for i, part in enumerate(re + im):
                    st[chunk(k * SUB, SUB, i), :] = part
            return 0

        lax.fori_loop(0, TILE // SUB, sub, 0, unroll=8)

        def scatter(g, _):
            at = [src[base + g * UNROLL + j] for j in range(UNROLL)]
            to = [rel[base + g * UNROLL + j] for j in range(UNROLL)]
            add_rows((gleft, at, staged(a_st, g)), (grel, to, staged(r_st, g)))
            return 0

        lax.fori_loop(0, groups, scatter, 0)
        return 0

    lax.fori_loop(0, (live + TILE - 1) // TILE, tile, 0)

    @pl.when(c == SPANS - 1)
    def _():
        rel_out[...] = grel[...].astype(BF16)
        adagrad_tables(gleft, left_t, state, new_ref, new_state)


def left_update(src, rel, live, source, relation, grad_product, left_t, state):
    smem = pl.BlockSpec(memory_space=pltpu.SMEM)
    vmem = pl.BlockSpec(memory_space=pltpu.VMEM)
    block = pl.BlockSpec((1, SPAN_PAD, 512), lambda c: (c, 0, 0))
    return pl.pallas_call(
        left_kernel,
        grid=(SPANS,),
        out_shape=[
            jax.ShapeDtypeStruct((WIDTH, ROWS), F32),
            jax.ShapeDtypeStruct((1, ROWS), F32),
            jax.ShapeDtypeStruct((REL_TALL, 128), BF16),
        ],
        in_specs=[smem] * 3 + [block] * 3 + [vmem] * 2,
        out_specs=[vmem] * 3,
        scratch_shapes=[pltpu.VMEM((4 * ROWS, 128), F32), pltpu.VMEM((REL_TALL, 128), F32)]
        + [pltpu.VMEM((4 * TILE, 128), F32)] * 2,
        compiler_params=pltpu.CompilerParams(**PARAMS),
        cost_estimate=pl.CostEstimate(flops=0, bytes_accessed=240_000_000, transcendentals=0),
        name="left_update",
    )(src, rel, live, source, relation, grad_product, left_t, state)


def right_kernel(ids, *refs):
    backs = refs[:PARTS]
    g_hbm, right_t, state, new_ref, new_state, total, stage, sem = refs[PARTS:]
    c = pl.program_id(0)

    @pl.when(c == 0)
    def _():
        copy = pltpu.make_async_copy(g_hbm, total.at[pl.ds(0, 4 * ROWS)], sem)
        copy.start()
        copy.wait()

    def unpack(back_ref, p, _):
        parts = unpack_wire(back_ref[p].astype(F32))
        for k, part in enumerate(parts):
            stage[chunk(p * SLOT, SLOT, k), :] = part
        return 0

    def scatter(p, _):
        base = p * (SPANS * SLOT) + c * SLOT

        def group(g, _):
            wanted = [ids[base + g * UNROLL + j] for j in range(UNROLL)]
            add_rows((total, wanted, staged(stage, p * (SLOT // UNROLL) + g)))
            return 0

        lax.fori_loop(0, SLOT // UNROLL, group, 0)
        return 0

    for k, back_ref in enumerate(backs):

        @pl.when(c // PART == k)
        def _():
            lax.fori_loop(0, PEERS, functools.partial(unpack, back_ref), 0, unroll=4)

    lax.fori_loop(0, PEERS, scatter, 0)

    @pl.when(c == SPANS - 1)
    def _():
        adagrad_tables(total, right_t, state, new_ref, new_state)


def right_update(ids, backs, grad, right_t, state):
    def part(k):
        return pl.BlockSpec(
            (PEERS, WIRE, 128), lambda c: (0, jnp.clip(c - k * PART, 0, PART - 1), 0)
        )

    vmem = pl.BlockSpec(memory_space=pltpu.VMEM)
    return pl.pallas_call(
        right_kernel,
        grid=(SPANS,),
        out_shape=[
            jax.ShapeDtypeStruct((WIDTH, ROWS), F32),
            jax.ShapeDtypeStruct((1, ROWS), F32),
        ],
        in_specs=[
            pl.BlockSpec(memory_space=pltpu.SMEM),
            *(part(k) for k in range(PARTS)),
            pl.BlockSpec(memory_space=pl.ANY),
            vmem,
            vmem,
        ],
        out_specs=[vmem] * 2,
        scratch_shapes=[
            pltpu.VMEM((TALL, 128), F32),
            pltpu.VMEM((PEERS * 4 * SLOT, 128), F32),
            pltpu.SemaphoreType.DMA,
        ],
        compiler_params=pltpu.CompilerParams(**PARAMS),
        cost_estimate=pl.CostEstimate(flops=0, bytes_accessed=160_000_000, transcendentals=0),
        name="right_update",
    )(ids, *backs, grad, right_t, state)


def places():
    grp, shard = lax.axis_index("grp"), lax.axis_index("shard")
    core, chip = lax.rem(grp, CORES), lax.div(grp, CORES)

    def other_core():
        return (chip * CORES + 1 - core, shard)

    def along_grp(d):
        return (lax.rem(chip + d, CHIPS) * CORES + core, shard)

    def along_shard(d):
        return (grp, lax.rem(shard + d, PEERS))

    return core, chip, shard, other_core, along_grp, along_shard


def greet(devices):
    barrier = pltpu.get_barrier_semaphore()
    for device in devices:
        pl.semaphore_signal(
            barrier, inc=1, device_id=device, device_id_type=pl.DeviceIdType.MESH
        )
    pl.semaphore_wait(barrier, len(devices))


def sender(sends, recvs):
    def send(src, dst, slot, to):
        copy = pltpu.make_async_remote_copy(
            src_ref=src, dst_ref=dst, send_sem=sends.at[slot], recv_sem=recvs.at[slot],
            device_id=to, device_id_type=pl.DeviceIdType.MESH,
        )
        copy.start()
        return copy

    return send


def relation_sum_kernel(mine, out, got_0, half, got_1, sends, recvs):
    core, chip, shard, other_core, along_grp, along_shard = places()
    steps = range(1, PEERS)
    greet([other_core()] + [along_shard(d) for d in steps])
    send = sender(sends, recvs)
    copy = send(mine.at[1 - core], got_0, 0, other_core())
    copy.wait()

    def add(p, _):
        half[p] = (mine[core, p].astype(F32) + got_0[p].astype(F32)).astype(BF16)
        return 0

    lax.fori_loop(0, PEERS, add, 0)
    copies = [
        send(half.at[lax.rem(shard + d, PEERS)], got_1.at[d - 1], d, along_shard(d))
        for d in steps
    ]
    for copy in copies:
        copy.wait()

    def total_of(k, _):
        total = mine[core, shard, k].astype(F32) + got_0[shard, k].astype(F32)
        for d in range(PEERS - 1):
            total = total + got_1[d, k].astype(F32)
        out[k] = total
        return 0

    lax.fori_loop(0, CHIPS, total_of, 0)


def relation_sum(grad):
    vmem = pl.BlockSpec(memory_space=pltpu.VMEM)
    return pl.pallas_call(
        relation_sum_kernel,
        out_shape=jax.ShapeDtypeStruct((CHIPS, REL_SHARE, 128), F32),
        in_specs=[vmem],
        out_specs=vmem,
        scratch_shapes=[
            pltpu.VMEM((PEERS, CHIPS, REL_SHARE, 128), BF16),
            pltpu.VMEM((PEERS, CHIPS, REL_SHARE, 128), BF16),
            pltpu.VMEM((PEERS - 1, CHIPS, REL_SHARE, 128), BF16),
            pltpu.SemaphoreType.DMA((8,)),
            pltpu.SemaphoreType.DMA((8,)),
        ],
        compiler_params=pltpu.CompilerParams(
            collective_id=0, has_side_effects=True, vmem_limit_bytes=32 * 1024 * 1024
        ),
        cost_estimate=pl.CostEstimate(flops=0, bytes_accessed=4_000_000, transcendentals=0),
        name="relation_sum",
    )(grad.reshape(CORES, PEERS, CHIPS, REL_SHARE, 128))


def relation_cross_kernel(mine, out, got, total, sends, recvs):
    core, chip, shard, other_core, along_grp, along_shard = places()
    steps = range(1, CHIPS)
    greet([along_grp(d) for d in steps])
    send = sender(sends, recvs)
    copies = [
        send(mine.at[lax.rem(chip + d, CHIPS)], got.at[d - 1], d - 1, along_grp(d))
        for d in steps
    ]
    for copy in copies:
        copy.wait()
    added = mine[chip]
    for d in range(CHIPS - 1):
        added = added + got[d]
    total[...] = added
    out[chip] = added
    copies = [send(total, out.at[chip], 6 + d, along_grp(d)) for d in steps]
    for copy in copies:
        copy.wait()


def relation_cross(share):
    vmem = pl.BlockSpec(memory_space=pltpu.VMEM)
    return pl.pallas_call(
        relation_cross_kernel,
        out_shape=jax.ShapeDtypeStruct((CHIPS, REL_SHARE, 128), F32),
        in_specs=[vmem],
        out_specs=vmem,
        scratch_shapes=[
            pltpu.VMEM((CHIPS - 1, REL_SHARE, 128), F32),
            pltpu.VMEM((REL_SHARE, 128), F32),
            pltpu.SemaphoreType.DMA((14,)),
            pltpu.SemaphoreType.DMA((14,)),
        ],
        compiler_params=pltpu.CompilerParams(
            collective_id=2, has_side_effects=True, vmem_limit_bytes=32 * 1024 * 1024
        ),
        cost_estimate=pl.CostEstimate(flops=0, bytes_accessed=4_000_000, transcendentals=0),
        name="relation_cross",
    )(share)


def relation_spread_kernel(mine, out, sends, recvs):
    core, chip, shard, other_core, along_grp, along_shard = places()
    steps = range(1, PEERS)
    greet([other_core()] + [along_shard(d) for d in steps])
    send = sender(sends, recvs)
    copies = [send(mine, out.at[core, shard], d, along_shard(d)) for d in steps]
    out[core, shard] = mine[...]
    across = [send(mine, out.at[core, shard], 8, other_core())]
    for d in steps:
        copies[d - 1].wait_recv()
        block = out.at[core, lax.rem(shard + PEERS - d, PEERS)]
        across.append(send(block, block, 8 + d, other_core()))
    for copy in copies:
        copy.wait_send()
    for copy in across:
        copy.wait()


def relation_spread(total):
    vmem = pl.BlockSpec(memory_space=pltpu.VMEM)
    out = pl.pallas_call(
        relation_spread_kernel,
        out_shape=jax.ShapeDtypeStruct((CORES, PEERS, CHIPS, REL_SHARE, 128), F32),
        in_specs=[vmem],
        out_specs=vmem,
        scratch_shapes=[pltpu.SemaphoreType.DMA((16,)), pltpu.SemaphoreType.DMA((16,))],
        compiler_params=pltpu.CompilerParams(
            collective_id=1, has_side_effects=True, vmem_limit_bytes=32 * 1024 * 1024
        ),
        cost_estimate=pl.CostEstimate(flops=0, bytes_accessed=4_000_000, transcendentals=0),
        name="relation_spread",
    )(total)
    return out.reshape(REL_TALL, 128)


def relation_kernel(g_ref, rel_t, state, new_ref, new_state):
    for i in range(RELS_PAD // 128):
        low, high = i * 128, min(RELS, i * 128 + 128)
        new, ns = adagrad_block(g_ref, rel_t[:, low : low + 128], state[:, low : low + 128], i)
        new_ref[:, low:high] = new[:, : high - low]
        new_state[:, low:high] = ns[:, : high - low]


def relation_update(grad, rel_t, state):
    vmem = pl.BlockSpec(memory_space=pltpu.VMEM)
    return pl.pallas_call(
        relation_kernel,
        out_shape=[
            jax.ShapeDtypeStruct((WIDTH, RELS), F32),
            jax.ShapeDtypeStruct((1, RELS), F32),
        ],
        in_specs=[vmem] * 3,
        out_specs=[vmem] * 2,
        compiler_params=pltpu.CompilerParams(**PARAMS),
        name="relation_update",
    )(grad, rel_t, state)


def passed_along(block, axis, distance):
    devices = range(lax.axis_size(axis))
    route = [((i - distance) % len(devices), i) for i in devices]
    return lax.ppermute(block, axis, route)


def exchange(x):
    return lax.all_to_all(x, "shard", split_axis=0, concat_axis=0, tiled=True)


def local(
    left_table, right_table, left_state, right_state, relations, relation_state,
    source_rows, relation_ids, target_rows, negative_rows, span_sizes,
):
    left_t, right_t = left_table.T, right_table.T
    wanted = negative_rows.reshape(SPANS, PEERS, NEG_PER).transpose(1, 0, 2)
    wanted = jnp.pad(wanted, ((0, 0), (0, 0), (0, SLOT - NEG_PER)), constant_values=DUMP)
    asked = exchange(wanted.reshape(PEERS, SPANS * SLOT)).reshape(-1)
    served = serve(asked, right_t)
    got = exchange(served)

    def flat(ids):
        return jnp.pad(ids, ((0, 0), (0, SPAN_PAD - ids.shape[1]))).reshape(-1)

    src, rel, tgt = flat(source_rows), flat(relation_ids), flat(target_rows)
    live = span_sizes.reshape(SPANS)
    rel_t = jnp.pad(relations.T, ((0, 0), (0, RELS_PAD - RELS)))
    rel_state = jnp.pad(relation_state, (0, RELS_PAD - RELS), constant_values=1.0)
    source, relation, product, pos_target, grad_right = forward(
        src, rel, tgt, live, left_t, right_t, rel_t
    )
    grad_product, returned = None, []
    for k in range(PARTS):
        grad_product, back = negatives(live, product, pos_target, got, k * PART, grad_product)
        returned.append(exchange(back))
    new_left, new_left_state, grad_rel = left_update(
        src, rel, live, source, relation, grad_product, left_t, left_state.reshape(1, ROWS)
    )
    sent_left, grad_rel = lax.optimization_barrier((new_left.astype(jnp.float16), grad_rel))
    moved_left = passed_along(sent_left, "grp", ROUND)
    rel_share = relation_sum(grad_rel)
    returned, rel_share = lax.optimization_barrier((returned, rel_share))
    new_right, new_right_state = right_update(
        asked, returned, grad_right, right_t, right_state.reshape(1, ROWS)
    )
    rel_share, sent = lax.optimization_barrier((rel_share, new_right.astype(jnp.float16)))
    rel_share = relation_cross(rel_share)
    rel_share, sent = lax.optimization_barrier((rel_share, sent))
    moved_right = passed_along(sent, "grp", ROUND)
    rel_total = relation_spread(rel_share)
    states = jnp.concatenate([new_left_state, new_right_state], 0)
    moved_states = passed_along(states, "grp", ROUND)
    new_rel, new_rel_state = relation_update(rel_total, rel_t, rel_state.reshape(1, RELS_PAD))
    new_rel, moved_left = lax.optimization_barrier((new_rel, moved_left))
    moved_right, moved_states = lax.optimization_barrier((moved_right, moved_states))
    return (
        moved_left.astype(F32).T,
        moved_states[0],
        moved_right.astype(F32).T,
        moved_states[1],
        new_rel.T,
        new_rel_state.reshape(RELS),
    )


def solution(mesh):
    rows, flat = P(("grp", "shard"), None), P(("grp", "shard"))
    return jax.shard_map(
        local,
        mesh=mesh,
        in_specs=(rows, rows, flat, flat, P(), P(), rows, rows, rows, rows, rows),
        out_specs=(rows, flat, rows, flat, P(), P()),
        check_vma=False,
    )
```

```python
import functools

import jax
import jax.numpy as jnp
from jax import lax
from jax.experimental import pallas as pl
from jax.experimental.pallas import tpu as pltpu
from jax.sharding import PartitionSpec as P

ROUND = 5
LEARN_RATE = 0.1
EPSILON = 1e-08

WIDTH = 400
HALF = 200
REST = HALF - 128
SPANS = 9
PEERS = 8
NEG_PER = 125
SLOT = 128
SPAN_PAD = 1024
ROWS = 4096
DUMP = ROWS
TALL = 4 * (ROWS + 8)
RELS = 1345
RELS_PAD = 1408
CORES = 2
CHIPS = 8
REL_SHARE = 48
REL_TALL = CORES * PEERS * CHIPS * REL_SHARE
BOUNDS = (0, 3, SPANS)
PARTS = len(BOUNDS) - 1
TILE = 256
SUB = 32
UNROLL = 16
CHUNKS = ((0, 128), (128, 200), (200, 328), (328, 400))
WIRE = 400

F32 = jnp.float32
BF16 = jnp.bfloat16
PARAMS = dict(vmem_limit_bytes=58 * 1024 * 1024)


def lane_ids(shape):
    return lax.broadcasted_iota(jnp.int32, shape, len(shape) - 1)


def to_rows(t_ref, out_ref, count):
    def block(i, _):
        at = pl.ds(pl.multiple_of(i * 128, 128), 128)
        for c, (low, high) in enumerate(CHUNKS):
            part = t_ref[low:high, at]
            if high - low < 128:
                part = jnp.concatenate([part, jnp.zeros((128 - (high - low), 128), F32)], 0)
            out_ref[pl.ds(i * 512 + c, 128, stride=4), :] = part.T
        return 0

    lax.fori_loop(0, count // 128, block, 0, unroll=8 if count == ROWS else 1)


def adagrad_block(g_refs, t, state, i):
    parts = []
    for c, (low, high) in enumerate(CHUNKS):
        at = pl.ds(i * 512 + c, 128, stride=4)
        part = g_refs[0][at, :]
        for g_ref in g_refs[1:]:
            part = part + g_ref[at, :]
        parts.append(part.T[: high - low])
    grad = jnp.concatenate(parts, 0)
    new_state = state + jnp.sum(grad * grad, 0, keepdims=True) * (1.0 / WIDTH)
    rate = LEARN_RATE / (jnp.sqrt(new_state) + EPSILON)
    return t - grad * rate, new_state


def adagrad_tables(g_refs, t_ref, state_ref, new_ref, new_state_ref):
    def block(i, _):
        at = pl.ds(pl.multiple_of(i * 128, 128), 128)
        new, state = adagrad_block(g_refs, t_ref[:, at], state_ref[:, at], i)
        new_ref[:, at] = new.astype(new_ref.dtype)
        new_state_ref[:, at] = state
        return 0

    lax.fori_loop(0, ROWS // 128, block, 0, unroll=2)


def spot(group, j):
    return pl.ds(group * (4 * UNROLL) + 4 * j, 4)


def chunk(first, count, c):
    return pl.ds(first * 4 + c, count, stride=4)


def row(index):
    return pl.ds(pl.multiple_of(index * 4, 4), 4)


def add_rows(*work):
    for j in range(len(work[0][1])):
        for refs, indices, values in work:
            ref, at = refs[j % len(refs)], row(indices[j])
            ref[at, :] = ref[at, :] + values[j]()


def staged(stage, group):
    return [functools.partial(lambda j: stage[spot(group, j), :], j) for j in range(UNROLL)]


def serve_kernel(ids, t_ref, out_ref, table, stage):
    peer = pl.program_id(0)

    @pl.when(peer == 0)
    def _():
        to_rows(t_ref, table, ROWS)
        table[4 * ROWS :, :] = jnp.zeros((TALL - 4 * ROWS, 128), F32)

    lanes = lane_ids((SLOT, 128))

    def span(c, _):
        base = peer * (SPANS * SLOT) + c * SLOT

        def group(g, _):
            for j in range(UNROLL):
                stage[spot(g, j), :] = table[row(ids[base + g * UNROLL + j]), :]
            return 0

        lax.fori_loop(0, SLOT // UNROLL, group, 0, unroll=8)
        re0, re1, im0, im1 = (stage[chunk(0, SLOT, k), :] for k in range(4))
        moved = pltpu.roll(im1, REST, 1)
        mixed = jnp.where(lanes < REST, re1, moved)
        tail = jnp.where(lanes < 16, moved, 0.0)
        packed = tail[:16]
        for k in range(1, 8):
            packed = packed + pltpu.roll(tail[16 * k : 16 * k + 16], 16 * k, 1)
        at = pl.multiple_of(c * WIRE, 16)
        out_ref[0, pl.ds(at, 128), :] = re0.astype(BF16)
        out_ref[0, pl.ds(at + 128, 128), :] = im0.astype(BF16)
        out_ref[0, pl.ds(at + 256, 128), :] = mixed.astype(BF16)
        out_ref[0, pl.ds(at + 384, 16), :] = packed.astype(BF16)
        return 0

    lax.fori_loop(0, SPANS, span, 0)


def serve(ids, table_t):
    return pl.pallas_call(
        serve_kernel,
        grid=(PEERS,),
        out_shape=jax.ShapeDtypeStruct((PEERS, SPANS * WIRE, 128), BF16),
        in_specs=[
            pl.BlockSpec(memory_space=pltpu.SMEM),
            pl.BlockSpec(memory_space=pltpu.VMEM),
        ],
        out_specs=pl.BlockSpec((1, SPANS * WIRE, 128), lambda p: (p, 0, 0)),
        scratch_shapes=[
            pltpu.VMEM((TALL, 128), F32),
            pltpu.VMEM((4 * SLOT, 128), F32),
        ],
        compiler_params=pltpu.CompilerParams(**PARAMS),
        cost_estimate=pl.CostEstimate(flops=0, bytes_accessed=80_000_000, transcendentals=0),
        name="serve",
    )(ids, table_t)


def unpack_wire(block):
    lanes = lane_ids((SLOT, 128))
    re0, im0, mixed, packed = block[:128], block[128:256], block[256:384], block[384:400]
    re1 = jnp.where(lanes < REST, mixed, 0.0)
    tail = jnp.concatenate([pltpu.roll(packed, (56 - 16 * k) % 128, 1) for k in range(8)], 0)
    im1 = jnp.where(lanes < 56, pltpu.roll(mixed, 56, 1), jnp.where(lanes < REST, tail, 0.0))
    return re0, re1, im0, im1


def forward_kernel(
    src, rel, tgt, live_ref, left_t, right_t, rel_t,
    s_out, b_out, p_out, pt_out, g_ref,
    left, right, rels, s_st, b_st, t_st, g_st,
):
    c = pl.program_id(0)

    @pl.when(c == 0)
    def _():
        to_rows(left_t, left, ROWS)
        to_rows(right_t, right, ROWS)
        to_rows(rel_t, rels, RELS_PAD)
        g_ref[...] = jnp.zeros_like(g_ref)
        for st in (s_st, b_st, t_st):
            st[...] = jnp.zeros_like(st)

    live = live_ref[c]

    def tile(t, _):
        base = c * SPAN_PAD + t * TILE
        left_over = jnp.minimum(live - t * TILE, TILE)
        groups = (left_over + UNROLL - 1) // UNROLL

        def gather(g, _):
            for j in range(UNROLL):
                e = base + g * UNROLL + j
                s_st[spot(g, j), :] = left[row(src[e]), :]
                b_st[spot(g, j), :] = rels[row(rel[e]), :]
                t_st[spot(g, j), :] = right[row(tgt[e]), :]
            return 0

        lax.fori_loop(0, groups, gather, 0)

        def sub(k, _):
            s, b, q = (
                [st[chunk(k * SUB, SUB, i), :] for i in range(4)] for st in (s_st, b_st, t_st)
            )
            re = [s[i] * b[i] - s[i + 2] * b[i + 2] for i in range(2)]
            im = [s[i] * b[i + 2] + s[i + 2] * b[i] for i in range(2)]
            prod = re + im
            positive = jnp.sum(
                prod[0] * q[0] + prod[1] * q[1] + prod[2] * q[2] + prod[3] * q[3],
                -1, keepdims=True,
            )
            where = k * SUB + lax.broadcasted_iota(jnp.int32, (SUB, 1), 0)
            pos_grad = jnp.where(where < left_over, -jax.nn.sigmoid(-positive), 0.0)
            for i in range(4):
                g_st[chunk(k * SUB, SUB, i), :] = pos_grad * prod[i]
            rows = pl.ds(pl.multiple_of(t * TILE + k * SUB, SUB), SUB)
            for i in range(4):
                lanes = slice(i * 128, i * 128 + 128)
                s_out[0, rows, lanes] = s[i].astype(BF16)
                b_out[0, rows, lanes] = b[i].astype(BF16)
                p_out[0, rows, lanes] = prod[i].astype(BF16)
                pt_out[0, rows, lanes] = (pos_grad * q[i]).astype(BF16)
            return 0

        lax.fori_loop(0, TILE // SUB, sub, 0, unroll=8)

        def scatter(g, _):
            ids = [tgt[base + g * UNROLL + j] for j in range(UNROLL)]
            add_rows(([g_ref], ids, staged(g_st, g)))
            return 0

        lax.fori_loop(0, groups, scatter, 0)
        return 0

    lax.fori_loop(0, (live + TILE - 1) // TILE, tile, 0)


def forward(src, rel, tgt, live, left_t, right_t, rel_t):
    smem = pl.BlockSpec(memory_space=pltpu.SMEM)
    vmem = pl.BlockSpec(memory_space=pltpu.VMEM)
    per_edge = jax.ShapeDtypeStruct((SPANS, SPAN_PAD, 512), BF16)
    block = pl.BlockSpec((1, SPAN_PAD, 512), lambda c: (c, 0, 0))
    stage = pltpu.VMEM((4 * TILE, 128), F32)
    return pl.pallas_call(
        forward_kernel,
        grid=(SPANS,),
        out_shape=[per_edge] * 4 + [jax.ShapeDtypeStruct((4 * ROWS, 128), F32)],
        in_specs=[smem] * 4 + [vmem] * 3,
        out_specs=[block] * 4 + [vmem],
        scratch_shapes=[
            pltpu.VMEM((4 * ROWS, 128), F32),
            pltpu.VMEM((4 * ROWS, 128), F32),
            pltpu.VMEM((4 * RELS_PAD, 128), F32),
        ]
        + [stage] * 4,
        compiler_params=pltpu.CompilerParams(**PARAMS),
        cost_estimate=pl.CostEstimate(flops=0, bytes_accessed=280_000_000, transcendentals=0),
        name="forward",
    )(src, rel, tgt, live, left_t, right_t, rel_t)


def negatives_kernel(first, live_ref, p_ref, pt_ref, got_ref, *rest):
    gp_ref, back_ref, neg, acc = rest[-4:]
    c = pl.program_id(0)
    live = live_ref[first + c]

    def unpack(p, _):
        block = got_ref[p].astype(F32)
        at = pl.ds(pl.multiple_of(p * SLOT, SLOT), SLOT)
        for k, part in enumerate(unpack_wire(block)):
            neg[at, k * 128 : k * 128 + 128] = part.astype(BF16)
        return 0

    lax.fori_loop(0, PEERS, unpack, 0, unroll=4)
    acc[...] = jnp.zeros_like(acc)

    def tile(t, _):
        rows = pl.ds(pl.multiple_of(t * TILE, TILE), TILE)
        product = p_ref[0, rows, :]
        scores = lax.dot_general(
            product, neg[...], (((1,), (1,)), ((), ())), preferred_element_type=F32
        )
        where = t * TILE + lax.broadcasted_iota(jnp.int32, (TILE, 1), 0)
        weight = (where < live).astype(F32) * 0.5
        grad = (weight * jnp.tanh(scores * 0.5) + weight).astype(BF16)
        gp = jnp.dot(grad, neg[...], preferred_element_type=F32)
        gp_ref[0, rows, :] = (gp + pt_ref[0, rows, :].astype(F32)).astype(BF16)
        acc[...] += lax.dot_general(
            grad, product, (((0,), (0,)), ((), ())), preferred_element_type=F32
        )
        return 0

    lax.fori_loop(0, (live + TILE - 1) // TILE, tile, 0)

    lanes = lane_ids((SLOT, 128))

    def pack(p, _):
        g = acc[pl.ds(pl.multiple_of(p * SLOT, SLOT), SLOT), :]
        re0, re1, im0, im1 = (g[:, k * 128 : k * 128 + 128] for k in range(4))
        moved = pltpu.roll(im1, REST, 1)
        tail = jnp.where(lanes < 16, moved, 0.0)
        packed = tail[:16]
        for k in range(1, 8):
            packed = packed + pltpu.roll(tail[16 * k : 16 * k + 16], 16 * k, 1)
        back_ref[p, 0:128, :] = re0.astype(BF16)
        back_ref[p, 128:256, :] = im0.astype(BF16)
        back_ref[p, 256:384, :] = jnp.where(lanes < REST, re1, moved).astype(BF16)
        back_ref[p, 384:400, :] = packed.astype(BF16)
        return 0

    lax.fori_loop(0, PEERS, pack, 0, unroll=4)


def negatives(live, product, pos_target, got, first, count, grad_product):
    block = pl.BlockSpec((1, SPAN_PAD, 512), lambda c: (first + c, 0, 0))
    wire = pl.BlockSpec((PEERS, WIRE, 128), lambda c: (0, first + c, 0))
    operands = [live, product, pos_target, got]
    specs = [pl.BlockSpec(memory_space=pltpu.SMEM), block, block, wire]
    aliases = {}
    if grad_product is not None:
        operands.append(grad_product)
        specs.append(pl.BlockSpec(memory_space=pl.ANY))
        aliases = {4: 0}
    return pl.pallas_call(
        functools.partial(negatives_kernel, first),
        grid=(count,),
        out_shape=[
            jax.ShapeDtypeStruct((SPANS, SPAN_PAD, 512), BF16),
            jax.ShapeDtypeStruct((PEERS, count * WIRE, 128), BF16),
        ],
        in_specs=specs,
        out_specs=[block, pl.BlockSpec((PEERS, WIRE, 128), lambda c: (0, c, 0))],
        scratch_shapes=[
            pltpu.VMEM((PEERS * SLOT, 512), BF16),
            pltpu.VMEM((PEERS * SLOT, 512), F32),
        ],
        input_output_aliases=aliases,
        compiler_params=pltpu.CompilerParams(**PARAMS),
        cost_estimate=pl.CostEstimate(
            flops=5_000_000_000 * count, bytes_accessed=15_000_000 * count, transcendentals=0
        ),
        name="negatives",
    )(*operands)


def left_kernel(
    src, rel, live_ref, s_ref, b_ref, gp_ref, left_t, state, new_ref, new_state, rel_out, *refs
):
    glefts, grels, (a_st, r_st) = refs[:2], refs[2:4], refs[4:]
    c = pl.program_id(0)

    @pl.when(c == 0)
    def _():
        for total in glefts + grels:
            total[...] = jnp.zeros_like(total)

    live = live_ref[c]

    def tile(t, _):
        base = c * SPAN_PAD + t * TILE
        groups = (jnp.minimum(live - t * TILE, TILE) + UNROLL - 1) // UNROLL

        def sub(k, _):
            rows = pl.ds(pl.multiple_of(t * TILE + k * SUB, SUB), SUB)
            s, b, g = (
                [ref[0, rows, i * 128 : i * 128 + 128].astype(F32) for i in range(4)]
                for ref in (s_ref, b_ref, gp_ref)
            )
            for st, o in ((a_st, b), (r_st, s)):
                re = [g[i] * o[i] + g[i + 2] * o[i + 2] for i in range(2)]
                im = [g[i + 2] * o[i] - g[i] * o[i + 2] for i in range(2)]
                for i, part in enumerate(re + im):
                    st[chunk(k * SUB, SUB, i), :] = part
            return 0

        lax.fori_loop(0, TILE // SUB, sub, 0, unroll=8)

        def scatter(g, _):
            at = [src[base + g * UNROLL + j] for j in range(UNROLL)]
            to = [rel[base + g * UNROLL + j] for j in range(UNROLL)]
            add_rows((glefts, at, staged(a_st, g)), (grels, to, staged(r_st, g)))
            return 0

        lax.fori_loop(0, groups, scatter, 0)
        return 0

    lax.fori_loop(0, (live + TILE - 1) // TILE, tile, 0)

    @pl.when(c == SPANS - 1)
    def _():
        rel_out[...] = (grels[0][...] + grels[1][...]).astype(BF16)
        adagrad_tables(glefts, left_t, state, new_ref, new_state)


def left_update(src, rel, live, source, relation, grad_product, left_t, state):
    smem = pl.BlockSpec(memory_space=pltpu.SMEM)
    vmem = pl.BlockSpec(memory_space=pltpu.VMEM)
    block = pl.BlockSpec((1, SPAN_PAD, 512), lambda c: (c, 0, 0))
    return pl.pallas_call(
        left_kernel,
        grid=(SPANS,),
        out_shape=[
            jax.ShapeDtypeStruct((WIDTH, ROWS), F32),
            jax.ShapeDtypeStruct((1, ROWS), F32),
            jax.ShapeDtypeStruct((REL_TALL, 128), BF16),
        ],
        in_specs=[smem] * 3 + [block] * 3 + [vmem] * 2,
        out_specs=[vmem] * 3,
        scratch_shapes=[pltpu.VMEM((4 * ROWS, 128), F32)] * 2
        + [pltpu.VMEM((REL_TALL, 128), F32)] * 2
        + [pltpu.VMEM((4 * TILE, 128), F32)] * 2,
        compiler_params=pltpu.CompilerParams(**PARAMS),
        cost_estimate=pl.CostEstimate(flops=0, bytes_accessed=240_000_000, transcendentals=0),
        name="left_update",
    )(src, rel, live, source, relation, grad_product, left_t, state)


def right_kernel(ids, *refs):
    backs = refs[:PARTS]
    g_hbm, right_t, state, new_ref, new_state, total, other, stage, sem = refs[PARTS:]
    c = pl.program_id(0)

    @pl.when(c == 0)
    def _():
        copy = pltpu.make_async_copy(g_hbm, total.at[pl.ds(0, 4 * ROWS)], sem)
        copy.start()
        other[...] = jnp.zeros_like(other)
        copy.wait()

    def unpack(back_ref, p, _):
        parts = unpack_wire(back_ref[p].astype(F32))
        for k, part in enumerate(parts):
            stage[chunk(p * SLOT, SLOT, k), :] = part
        return 0

    def scatter(p, _):
        base = p * (SPANS * SLOT) + c * SLOT

        def group(g, _):
            wanted = [ids[base + g * UNROLL + j] for j in range(UNROLL)]
            add_rows(([total, other], wanted, staged(stage, p * (SLOT // UNROLL) + g)))
            return 0

        lax.fori_loop(0, SLOT // UNROLL, group, 0)
        return 0

    for k, back_ref in enumerate(backs):

        @pl.when((c >= BOUNDS[k]) & (c < BOUNDS[k + 1]))
        def _():
            lax.fori_loop(0, PEERS, functools.partial(unpack, back_ref), 0, unroll=4)

    lax.fori_loop(0, PEERS, scatter, 0)

    @pl.when(c == SPANS - 1)
    def _():
        adagrad_tables([total, other], right_t, state, new_ref, new_state)


def right_update(ids, backs, grad, right_t, state):
    def part(k):
        return pl.BlockSpec(
            (PEERS, WIRE, 128),
            lambda c: (0, jnp.clip(c - BOUNDS[k], 0, BOUNDS[k + 1] - BOUNDS[k] - 1), 0),
        )

    vmem = pl.BlockSpec(memory_space=pltpu.VMEM)
    return pl.pallas_call(
        right_kernel,
        grid=(SPANS,),
        out_shape=[
            jax.ShapeDtypeStruct((WIDTH, ROWS), F32),
            jax.ShapeDtypeStruct((1, ROWS), F32),
        ],
        in_specs=[
            pl.BlockSpec(memory_space=pltpu.SMEM),
            *(part(k) for k in range(PARTS)),
            pl.BlockSpec(memory_space=pl.ANY),
            vmem,
            vmem,
        ],
        out_specs=[vmem] * 2,
        scratch_shapes=[
            pltpu.VMEM((TALL, 128), F32),
            pltpu.VMEM((TALL, 128), F32),
            pltpu.VMEM((PEERS * 4 * SLOT, 128), F32),
            pltpu.SemaphoreType.DMA,
        ],
        compiler_params=pltpu.CompilerParams(**PARAMS),
        cost_estimate=pl.CostEstimate(flops=0, bytes_accessed=4_000_000, transcendentals=0),
        name="right_update",
    )(ids, *backs, grad, right_t, state)


def places():
    grp, shard = lax.axis_index("grp"), lax.axis_index("shard")
    core, chip = lax.rem(grp, CORES), lax.div(grp, CORES)

    def other_core():
        return (chip * CORES + 1 - core, shard)

    def along_grp(d):
        return (lax.rem(chip + d, CHIPS) * CORES + core, shard)

    def along_shard(d):
        return (grp, lax.rem(shard + d, PEERS))

    return core, chip, shard, other_core, along_grp, along_shard


def greet(devices):
    barrier = pltpu.get_barrier_semaphore()
    for device in devices:
        pl.semaphore_signal(
            barrier, inc=1, device_id=device, device_id_type=pl.DeviceIdType.MESH
        )
    pl.semaphore_wait(barrier, len(devices))


def sender(sends, recvs):
    def send(src, dst, slot, to):
        copy = pltpu.make_async_remote_copy(
            src_ref=src, dst_ref=dst, send_sem=sends.at[slot], recv_sem=recvs.at[slot],
            device_id=to, device_id_type=pl.DeviceIdType.MESH,
        )
        copy.start()
        return copy

    return send


def relation_sum_kernel(mine, out, got_0, half, got_1, sum_1, got_2, sum_2, sends, recvs):
    core, chip, shard, other_core, along_grp, along_shard = places()
    steps = range(1, PEERS)
    greet(
        [other_core()] + [along_shard(d) for d in steps] + [along_grp(d) for d in steps]
    )
    send = sender(sends, recvs)
    copy = send(mine.at[1 - core], got_0, 0, other_core())
    copy.wait()

    def add(p, _):
        half[p] = (mine[core, p].astype(F32) + got_0[p].astype(F32)).astype(BF16)
        return 0

    lax.fori_loop(0, PEERS, add, 0)
    copies = [
        send(half.at[lax.rem(shard + d, PEERS)], got_1.at[d - 1], d, along_shard(d))
        for d in steps
    ]
    for copy in copies:
        copy.wait()

    def total_of(k, _):
        total = mine[core, shard, k].astype(F32) + got_0[shard, k].astype(F32)
        for d in range(PEERS - 1):
            total = total + got_1[d, k].astype(F32)
        sum_1[k] = total
        return 0

    lax.fori_loop(0, CHIPS, total_of, 0)
    copies = [
        send(sum_1.at[lax.rem(chip + d, CHIPS)], got_2.at[d - 1], 7 + d, along_grp(d))
        for d in steps
    ]
    for copy in copies:
        copy.wait()
    total = sum_1[chip]
    for d in range(CHIPS - 1):
        total = total + got_2[d]
    sum_2[...] = total
    out[chip] = total
    copies = [send(sum_2, out.at[chip], 14 + d, along_grp(d)) for d in steps]
    for copy in copies:
        copy.wait()


def relation_sum(grad):
    vmem = pl.BlockSpec(memory_space=pltpu.VMEM)
    return pl.pallas_call(
        relation_sum_kernel,
        out_shape=jax.ShapeDtypeStruct((CHIPS, REL_SHARE, 128), F32),
        in_specs=[vmem],
        out_specs=vmem,
        scratch_shapes=[
            pltpu.VMEM((PEERS, CHIPS, REL_SHARE, 128), BF16),
            pltpu.VMEM((PEERS, CHIPS, REL_SHARE, 128), BF16),
            pltpu.VMEM((PEERS - 1, CHIPS, REL_SHARE, 128), BF16),
            pltpu.VMEM((CHIPS, REL_SHARE, 128), F32),
            pltpu.VMEM((CHIPS - 1, REL_SHARE, 128), F32),
            pltpu.VMEM((REL_SHARE, 128), F32),
            pltpu.SemaphoreType.DMA((22,)),
            pltpu.SemaphoreType.DMA((22,)),
        ],
        compiler_params=pltpu.CompilerParams(
            collective_id=0, has_side_effects=True, vmem_limit_bytes=32 * 1024 * 1024
        ),
        cost_estimate=pl.CostEstimate(flops=0, bytes_accessed=4_000_000, transcendentals=0),
        name="relation_sum",
    )(grad.reshape(CORES, PEERS, CHIPS, REL_SHARE, 128))


def relation_spread_kernel(mine, out, sends, recvs):
    core, chip, shard, other_core, along_grp, along_shard = places()
    steps = range(1, PEERS)
    greet([other_core()] + [along_shard(d) for d in steps])
    send = sender(sends, recvs)
    copies = [send(mine, out.at[core, shard], d, along_shard(d)) for d in steps]
    out[core, shard] = mine[...]
    across = [send(mine, out.at[core, shard], 8, other_core())]
    for d in steps:
        copies[d - 1].wait_recv()
        block = out.at[core, lax.rem(shard + PEERS - d, PEERS)]
        across.append(send(block, block, 8 + d, other_core()))
    for copy in copies:
        copy.wait_send()
    for copy in across:
        copy.wait()


def relation_spread(total):
    vmem = pl.BlockSpec(memory_space=pltpu.VMEM)
    out = pl.pallas_call(
        relation_spread_kernel,
        out_shape=jax.ShapeDtypeStruct((CORES, PEERS, CHIPS, REL_SHARE, 128), F32),
        in_specs=[vmem],
        out_specs=vmem,
        scratch_shapes=[pltpu.SemaphoreType.DMA((16,)), pltpu.SemaphoreType.DMA((16,))],
        compiler_params=pltpu.CompilerParams(
            collective_id=1, has_side_effects=True, vmem_limit_bytes=32 * 1024 * 1024
        ),
        cost_estimate=pl.CostEstimate(flops=0, bytes_accessed=4_000_000, transcendentals=0),
        name="relation_spread",
    )(total)
    return out.reshape(REL_TALL, 128)


def relation_kernel(g_ref, rel_t, state, new_ref, new_state):
    for i in range(RELS_PAD // 128):
        low, high = i * 128, min(RELS, i * 128 + 128)
        new, ns = adagrad_block([g_ref], rel_t[:, low : low + 128], state[:, low : low + 128], i)
        new_ref[:, low:high] = new[:, : high - low]
        new_state[:, low:high] = ns[:, : high - low]


def relation_update(grad, rel_t, state):
    vmem = pl.BlockSpec(memory_space=pltpu.VMEM)
    return pl.pallas_call(
        relation_kernel,
        out_shape=[
            jax.ShapeDtypeStruct((WIDTH, RELS), F32),
            jax.ShapeDtypeStruct((1, RELS), F32),
        ],
        in_specs=[vmem] * 3,
        out_specs=[vmem] * 2,
        compiler_params=pltpu.CompilerParams(**PARAMS),
        name="relation_update",
    )(grad, rel_t, state)


def passed_along(block, axis, distance):
    devices = range(lax.axis_size(axis))
    route = [((i - distance) % len(devices), i) for i in devices]
    return lax.ppermute(block, axis, route)


def exchange(x):
    return lax.all_to_all(x, "shard", split_axis=0, concat_axis=0, tiled=True)


def local(
    left_table, right_table, left_state, right_state, relations, relation_state,
    source_rows, relation_ids, target_rows, negative_rows, span_sizes,
):
    left_t, right_t = left_table.T, right_table.T
    wanted = negative_rows.reshape(SPANS, PEERS, NEG_PER).transpose(1, 0, 2)
    wanted = jnp.pad(wanted, ((0, 0), (0, 0), (0, SLOT - NEG_PER)), constant_values=DUMP)
    asked = exchange(wanted.reshape(PEERS, SPANS * SLOT)).reshape(-1)
    served = serve(asked, right_t)
    got = exchange(served)

    def flat(ids):
        return jnp.pad(ids, ((0, 0), (0, SPAN_PAD - ids.shape[1]))).reshape(-1)

    src, rel, tgt = flat(source_rows), flat(relation_ids), flat(target_rows)
    live = span_sizes.reshape(SPANS)
    rel_t = jnp.pad(relations.T, ((0, 0), (0, RELS_PAD - RELS)))
    rel_state = jnp.pad(relation_state, (0, RELS_PAD - RELS), constant_values=1.0)
    source, relation, product, pos_target, grad_right = forward(
        src, rel, tgt, live, left_t, right_t, rel_t
    )
    grad_product, returned = None, []
    for first, end in zip(BOUNDS, BOUNDS[1:]):
        grad_product, back = negatives(
            live, product, pos_target, got, first, end - first, grad_product
        )
        if returned:
            returned[-1], back = lax.optimization_barrier((returned[-1], back))
        returned.append(exchange(back))
    new_left, new_left_state, grad_rel = left_update(
        src, rel, live, source, relation, grad_product, left_t, left_state.reshape(1, ROWS)
    )
    moved_left = passed_along(new_left.astype(jnp.float16), "grp", ROUND)
    new_right, new_right_state = right_update(
        asked, returned, grad_right, right_t, right_state.reshape(1, ROWS)
    )
    grad_rel, sent = lax.optimization_barrier((grad_rel, new_right.astype(jnp.float16)))
    rel_share = relation_sum(grad_rel)
    rel_share, sent = lax.optimization_barrier((rel_share, sent))
    moved_right = passed_along(sent, "grp", ROUND)
    rel_total = relation_spread(rel_share)
    states = jnp.concatenate([new_left_state, new_right_state], 0)
    moved_states = passed_along(states, "grp", ROUND)
    held_left, rel_total = lax.optimization_barrier((moved_left.astype(F32), rel_total))
    new_rel, new_rel_state = relation_update(rel_total, rel_t, rel_state.reshape(1, RELS_PAD))
    moved_right, moved_states, new_rel = lax.optimization_barrier(
        (moved_right, moved_states, new_rel)
    )
    return (
        held_left.T,
        moved_states[0],
        moved_right.astype(F32).T,
        moved_states[1],
        new_rel.T,
        new_rel_state.reshape(RELS),
    )


def solution(mesh):
    rows, flat = P(("grp", "shard"), None), P(("grp", "shard"))
    return jax.shard_map(
        local,
        mesh=mesh,
        in_specs=(rows, rows, flat, flat, P(), P(), rows, rows, rows, rows, rows),
        out_specs=(rows, flat, rows, flat, P(), P()),
        check_vma=False,
    )
```

```python
import functools

import jax
import jax.numpy as jnp
from jax import lax
from jax.experimental import pallas as pl
from jax.experimental.pallas import tpu as pltpu
from jax.sharding import PartitionSpec as P

ROUND = 5
LEARN_RATE = 0.1
EPSILON = 1e-08

WIDTH = 400
HALF = 200
REST = HALF - 128
SPANS = 9
PEERS = 8
NEG_PER = 125
SLOT = 128
SPAN_PAD = 1024
ROWS = 4096
DUMP = ROWS
TALL = 4 * (ROWS + 8)
RELS = 1345
RELS_PAD = 1408
CORES = 2
CHIPS = 8
REL_SHARE = 48
REL_TALL = CORES * PEERS * CHIPS * REL_SHARE
BOUNDS = (0, 3, SPANS)
PARTS = len(BOUNDS) - 1
TILE = 256
SUB = 32
UNROLL = 16
CHUNKS = ((0, 128), (128, 200), (200, 328), (328, 400))
WIRE = 400

F32 = jnp.float32
BF16 = jnp.bfloat16
PARAMS = dict(vmem_limit_bytes=58 * 1024 * 1024)


def lane_ids(shape):
    return lax.broadcasted_iota(jnp.int32, shape, len(shape) - 1)


def to_rows(t_ref, out_ref, count):
    def block(i, _):
        at = pl.ds(pl.multiple_of(i * 128, 128), 128)
        for c, (low, high) in enumerate(CHUNKS):
            part = t_ref[low:high, at]
            if high - low < 128:
                part = jnp.concatenate([part, jnp.zeros((128 - (high - low), 128), F32)], 0)
            out_ref[pl.ds(i * 512 + c, 128, stride=4), :] = part.T
        return 0

    lax.fori_loop(0, count // 128, block, 0, unroll=8 if count == ROWS else 1)


def adagrad_block(g_refs, t, state, i):
    parts = []
    for c, (low, high) in enumerate(CHUNKS):
        at = pl.ds(i * 512 + c, 128, stride=4)
        part = g_refs[0][at, :]
        for g_ref in g_refs[1:]:
            part = part + g_ref[at, :]
        parts.append(part.T[: high - low])
    grad = jnp.concatenate(parts, 0)
    new_state = state + jnp.sum(grad * grad, 0, keepdims=True) * (1.0 / WIDTH)
    rate = LEARN_RATE / (jnp.sqrt(new_state) + EPSILON)
    return t - grad * rate, new_state


def adagrad_tables(g_refs, t_ref, state_ref, new_ref, new_state_ref):
    def block(i, _):
        at = pl.ds(pl.multiple_of(i * 128, 128), 128)
        new, state = adagrad_block(g_refs, t_ref[:, at], state_ref[:, at], i)
        new_ref[:, at] = new.astype(new_ref.dtype)
        new_state_ref[:, at] = state
        return 0

    lax.fori_loop(0, ROWS // 128, block, 0, unroll=2)


def spot(group, j):
    return pl.ds(group * (4 * UNROLL) + 4 * j, 4)


def chunk(first, count, c):
    return pl.ds(first * 4 + c, count, stride=4)


def row(index):
    return pl.ds(pl.multiple_of(index * 4, 4), 4)


def add_rows(*work):
    for j in range(len(work[0][1])):
        for refs, indices, values in work:
            ref, at = refs[j % len(refs)], row(indices[j])
            ref[at, :] = ref[at, :] + values[j]()


def staged(stage, group):
    return [functools.partial(lambda j: stage[spot(group, j), :], j) for j in range(UNROLL)]


def serve_kernel(ids, t_ref, out_ref, table, stage):
    peer = pl.program_id(0)

    @pl.when(peer == 0)
    def _():
        to_rows(t_ref, table, ROWS)
        table[4 * ROWS :, :] = jnp.zeros((TALL - 4 * ROWS, 128), F32)

    lanes = lane_ids((SLOT, 128))

    def span(c, _):
        base = peer * (SPANS * SLOT) + c * SLOT

        def group(g, _):
            for j in range(UNROLL):
                stage[spot(g, j), :] = table[row(ids[base + g * UNROLL + j]), :]
            return 0

        lax.fori_loop(0, SLOT // UNROLL, group, 0, unroll=8)
        re0, re1, im0, im1 = (stage[chunk(0, SLOT, k), :] for k in range(4))
        moved = pltpu.roll(im1, REST, 1)
        mixed = jnp.where(lanes < REST, re1, moved)
        tail = jnp.where(lanes < 16, moved, 0.0)
        packed = tail[:16]
        for k in range(1, 8):
            packed = packed + pltpu.roll(tail[16 * k : 16 * k + 16], 16 * k, 1)
        at = pl.multiple_of(c * WIRE, 16)
        out_ref[0, pl.ds(at, 128), :] = re0.astype(BF16)
        out_ref[0, pl.ds(at + 128, 128), :] = im0.astype(BF16)
        out_ref[0, pl.ds(at + 256, 128), :] = mixed.astype(BF16)
        out_ref[0, pl.ds(at + 384, 16), :] = packed.astype(BF16)
        return 0

    lax.fori_loop(0, SPANS, span, 0)


def serve(ids, table_t):
    return pl.pallas_call(
        serve_kernel,
        grid=(PEERS,),
        out_shape=jax.ShapeDtypeStruct((PEERS, SPANS * WIRE, 128), BF16),
        in_specs=[
            pl.BlockSpec(memory_space=pltpu.SMEM),
            pl.BlockSpec(memory_space=pltpu.VMEM),
        ],
        out_specs=pl.BlockSpec((1, SPANS * WIRE, 128), lambda p: (p, 0, 0)),
        scratch_shapes=[
            pltpu.VMEM((TALL, 128), F32),
            pltpu.VMEM((4 * SLOT, 128), F32),
        ],
        compiler_params=pltpu.CompilerParams(**PARAMS),
        cost_estimate=pl.CostEstimate(flops=0, bytes_accessed=80_000_000, transcendentals=0),
        name="serve",
    )(ids, table_t)


def unpack_wire(block):
    lanes = lane_ids((SLOT, 128))
    re0, im0, mixed, packed = block[:128], block[128:256], block[256:384], block[384:400]
    re1 = jnp.where(lanes < REST, mixed, 0.0)
    tail = jnp.concatenate([pltpu.roll(packed, (56 - 16 * k) % 128, 1) for k in range(8)], 0)
    im1 = jnp.where(lanes < 56, pltpu.roll(mixed, 56, 1), jnp.where(lanes < REST, tail, 0.0))
    return re0, re1, im0, im1


def forward_kernel(
    src, rel, tgt, live_ref, left_t, right_t, rel_t,
    s_out, b_out, p_out, pt_out, g_ref,
    left, right, rels, s_st, b_st, t_st, g_st,
):
    c = pl.program_id(0)

    @pl.when(c == 0)
    def _():
        to_rows(left_t, left, ROWS)
        to_rows(right_t, right, ROWS)
        to_rows(rel_t, rels, RELS_PAD)
        g_ref[...] = jnp.zeros_like(g_ref)
        for st in (s_st, b_st, t_st):
            st[...] = jnp.zeros_like(st)

    live = live_ref[c]

    def tile(t, _):
        base = c * SPAN_PAD + t * TILE
        left_over = jnp.minimum(live - t * TILE, TILE)
        groups = (left_over + UNROLL - 1) // UNROLL

        def gather(g, _):
            for j in range(UNROLL):
                e = base + g * UNROLL + j
                s_st[spot(g, j), :] = left[row(src[e]), :]
                b_st[spot(g, j), :] = rels[row(rel[e]), :]
                t_st[spot(g, j), :] = right[row(tgt[e]), :]
            return 0

        lax.fori_loop(0, groups, gather, 0)

        def sub(k, _):
            s, b, q = (
                [st[chunk(k * SUB, SUB, i), :] for i in range(4)] for st in (s_st, b_st, t_st)
            )
            re = [s[i] * b[i] - s[i + 2] * b[i + 2] for i in range(2)]
            im = [s[i] * b[i + 2] + s[i + 2] * b[i] for i in range(2)]
            prod = re + im
            positive = jnp.sum(
                prod[0] * q[0] + prod[1] * q[1] + prod[2] * q[2] + prod[3] * q[3],
                -1, keepdims=True,
            )
            where = k * SUB + lax.broadcasted_iota(jnp.int32, (SUB, 1), 0)
            pos_grad = jnp.where(where < left_over, -jax.nn.sigmoid(-positive), 0.0)
            for i in range(4):
                g_st[chunk(k * SUB, SUB, i), :] = pos_grad * prod[i]
            rows = pl.ds(pl.multiple_of(t * TILE + k * SUB, SUB), SUB)
            for i in range(4):
                lanes = slice(i * 128, i * 128 + 128)
                s_out[0, rows, lanes] = s[i].astype(BF16)
                b_out[0, rows, lanes] = b[i].astype(BF16)
                p_out[0, rows, lanes] = prod[i].astype(BF16)
                pt_out[0, rows, lanes] = (pos_grad * q[i]).astype(BF16)
            return 0

        lax.fori_loop(0, TILE // SUB, sub, 0, unroll=8)

        def scatter(g, _):
            ids = [tgt[base + g * UNROLL + j] for j in range(UNROLL)]
            add_rows(([g_ref], ids, staged(g_st, g)))
            return 0

        lax.fori_loop(0, groups, scatter, 0)
        return 0

    lax.fori_loop(0, (live + TILE - 1) // TILE, tile, 0)


def forward(src, rel, tgt, live, left_t, right_t, rel_t):
    smem = pl.BlockSpec(memory_space=pltpu.SMEM)
    vmem = pl.BlockSpec(memory_space=pltpu.VMEM)
    per_edge = jax.ShapeDtypeStruct((SPANS, SPAN_PAD, 512), BF16)
    block = pl.BlockSpec((1, SPAN_PAD, 512), lambda c: (c, 0, 0))
    stage = pltpu.VMEM((4 * TILE, 128), F32)
    return pl.pallas_call(
        forward_kernel,
        grid=(SPANS,),
        out_shape=[per_edge] * 4 + [jax.ShapeDtypeStruct((4 * ROWS, 128), F32)],
        in_specs=[smem] * 4 + [vmem] * 3,
        out_specs=[block] * 4 + [vmem],
        scratch_shapes=[
            pltpu.VMEM((4 * ROWS, 128), F32),
            pltpu.VMEM((4 * ROWS, 128), F32),
            pltpu.VMEM((4 * RELS_PAD, 128), F32),
        ]
        + [stage] * 4,
        compiler_params=pltpu.CompilerParams(**PARAMS),
        cost_estimate=pl.CostEstimate(flops=0, bytes_accessed=280_000_000, transcendentals=0),
        name="forward",
    )(src, rel, tgt, live, left_t, right_t, rel_t)


def negatives_kernel(first, live_ref, p_ref, pt_ref, got_ref, *rest):
    gp_ref, back_ref, neg, acc = rest[-4:]
    c = pl.program_id(0)
    live = live_ref[first + c]

    def unpack(p, _):
        block = got_ref[p].astype(F32)
        at = pl.ds(pl.multiple_of(p * SLOT, SLOT), SLOT)
        for k, part in enumerate(unpack_wire(block)):
            neg[at, k * 128 : k * 128 + 128] = part.astype(BF16)
        return 0

    lax.fori_loop(0, PEERS, unpack, 0, unroll=4)
    acc[...] = jnp.zeros_like(acc)

    def tile(t, _):
        rows = pl.ds(pl.multiple_of(t * TILE, TILE), TILE)
        product = p_ref[0, rows, :]
        scores = lax.dot_general(
            product, neg[...], (((1,), (1,)), ((), ())), preferred_element_type=F32
        )
        where = t * TILE + lax.broadcasted_iota(jnp.int32, (TILE, 1), 0)
        weight = (where < live).astype(F32) * 0.5
        grad = (weight * jnp.tanh(scores * 0.5) + weight).astype(BF16)
        gp = jnp.dot(grad, neg[...], preferred_element_type=F32)
        gp_ref[0, rows, :] = (gp + pt_ref[0, rows, :].astype(F32)).astype(BF16)
        acc[...] += lax.dot_general(
            grad, product, (((0,), (0,)), ((), ())), preferred_element_type=F32
        )
        return 0

    lax.fori_loop(0, (live + TILE - 1) // TILE, tile, 0)

    lanes = lane_ids((SLOT, 128))

    def pack(p, _):
        g = acc[pl.ds(pl.multiple_of(p * SLOT, SLOT), SLOT), :]
        re0, re1, im0, im1 = (g[:, k * 128 : k * 128 + 128] for k in range(4))
        moved = pltpu.roll(im1, REST, 1)
        tail = jnp.where(lanes < 16, moved, 0.0)
        packed = tail[:16]
        for k in range(1, 8):
            packed = packed + pltpu.roll(tail[16 * k : 16 * k + 16], 16 * k, 1)
        back_ref[p, 0:128, :] = re0.astype(BF16)
        back_ref[p, 128:256, :] = im0.astype(BF16)
        back_ref[p, 256:384, :] = jnp.where(lanes < REST, re1, moved).astype(BF16)
        back_ref[p, 384:400, :] = packed.astype(BF16)
        return 0

    lax.fori_loop(0, PEERS, pack, 0, unroll=4)


def negatives(live, product, pos_target, got, first, count, grad_product):
    block = pl.BlockSpec((1, SPAN_PAD, 512), lambda c: (first + c, 0, 0))
    wire = pl.BlockSpec((PEERS, WIRE, 128), lambda c: (0, first + c, 0))
    operands = [live, product, pos_target, got]
    specs = [pl.BlockSpec(memory_space=pltpu.SMEM), block, block, wire]
    aliases = {}
    if grad_product is not None:
        operands.append(grad_product)
        specs.append(pl.BlockSpec(memory_space=pl.ANY))
        aliases = {4: 0}
    return pl.pallas_call(
        functools.partial(negatives_kernel, first),
        grid=(count,),
        out_shape=[
            jax.ShapeDtypeStruct((SPANS, SPAN_PAD, 512), BF16),
            jax.ShapeDtypeStruct((PEERS, count * WIRE, 128), BF16),
        ],
        in_specs=specs,
        out_specs=[block, pl.BlockSpec((PEERS, WIRE, 128), lambda c: (0, c, 0))],
        scratch_shapes=[
            pltpu.VMEM((PEERS * SLOT, 512), BF16),
            pltpu.VMEM((PEERS * SLOT, 512), F32),
        ],
        input_output_aliases=aliases,
        compiler_params=pltpu.CompilerParams(**PARAMS),
        cost_estimate=pl.CostEstimate(
            flops=5_000_000_000 * count, bytes_accessed=15_000_000 * count, transcendentals=0
        ),
        name="negatives",
    )(*operands)


def left_kernel(
    src, rel, live_ref, s_ref, b_ref, gp_ref, left_hbm, state, new_ref, new_state, rel_out, *refs
):
    glefts, grels, (a_st, r_st, left_t, sem) = refs[:2], refs[2:4], refs[4:]
    table = pltpu.make_async_copy(left_hbm, left_t, sem)
    c = pl.program_id(0)

    @pl.when(c == 0)
    def _():
        table.start()
        for total in glefts + grels:
            total[...] = jnp.zeros_like(total)

    live = live_ref[c]

    def tile(t, _):
        base = c * SPAN_PAD + t * TILE
        groups = (jnp.minimum(live - t * TILE, TILE) + UNROLL - 1) // UNROLL

        def sub(k, _):
            rows = pl.ds(pl.multiple_of(t * TILE + k * SUB, SUB), SUB)
            s, b, g = (
                [ref[0, rows, i * 128 : i * 128 + 128].astype(F32) for i in range(4)]
                for ref in (s_ref, b_ref, gp_ref)
            )
            for st, o in ((a_st, b), (r_st, s)):
                re = [g[i] * o[i] + g[i + 2] * o[i + 2] for i in range(2)]
                im = [g[i + 2] * o[i] - g[i] * o[i + 2] for i in range(2)]
                for i, part in enumerate(re + im):
                    st[chunk(k * SUB, SUB, i), :] = part
            return 0

        lax.fori_loop(0, TILE // SUB, sub, 0, unroll=8)

        def scatter(g, _):
            at = [src[base + g * UNROLL + j] for j in range(UNROLL)]
            to = [rel[base + g * UNROLL + j] for j in range(UNROLL)]
            add_rows((glefts, at, staged(a_st, g)), (grels, to, staged(r_st, g)))
            return 0

        lax.fori_loop(0, groups, scatter, 0)
        return 0

    lax.fori_loop(0, (live + TILE - 1) // TILE, tile, 0)

    @pl.when(c == SPANS - 1)
    def _():
        rel_out[...] = (grels[0][...] + grels[1][...]).astype(BF16)
        table.wait()
        adagrad_tables(glefts, left_t, state, new_ref, new_state)


def left_update(src, rel, live, source, relation, grad_product, left_t, state):
    smem = pl.BlockSpec(memory_space=pltpu.SMEM)
    vmem = pl.BlockSpec(memory_space=pltpu.VMEM)
    block = pl.BlockSpec((1, SPAN_PAD, 512), lambda c: (c, 0, 0))
    return pl.pallas_call(
        left_kernel,
        grid=(SPANS,),
        out_shape=[
            jax.ShapeDtypeStruct((WIDTH, ROWS), F32),
            jax.ShapeDtypeStruct((1, ROWS), F32),
            jax.ShapeDtypeStruct((REL_TALL, 128), BF16),
        ],
        in_specs=[smem] * 3 + [block] * 3 + [pl.BlockSpec(memory_space=pl.ANY), vmem],
        out_specs=[vmem] * 3,
        scratch_shapes=[pltpu.VMEM((4 * ROWS, 128), F32)] * 2
        + [pltpu.VMEM((REL_TALL, 128), F32)] * 2
        + [pltpu.VMEM((4 * TILE, 128), F32)] * 2
        + [pltpu.VMEM((WIDTH, ROWS), F32), pltpu.SemaphoreType.DMA],
        compiler_params=pltpu.CompilerParams(**PARAMS),
        cost_estimate=pl.CostEstimate(flops=0, bytes_accessed=240_000_000, transcendentals=0),
        name="left_update",
    )(src, rel, live, source, relation, grad_product, left_t, state)


def right_kernel(ids, *refs):
    backs = refs[:PARTS]
    g_hbm, right_hbm, state, new_ref, new_state = refs[PARTS : PARTS + 5]
    total, other, stage, sem, right_t, table_sem = refs[PARTS + 5 :]
    table = pltpu.make_async_copy(right_hbm, right_t, table_sem)
    c = pl.program_id(0)

    @pl.when(c == 0)
    def _():
        copy = pltpu.make_async_copy(g_hbm, total.at[pl.ds(0, 4 * ROWS)], sem)
        copy.start()
        other[...] = jnp.zeros_like(other)
        copy.wait()
        table.start()

    def unpack(back_ref, p, _):
        parts = unpack_wire(back_ref[p].astype(F32))
        for k, part in enumerate(parts):
            stage[chunk(p * SLOT, SLOT, k), :] = part
        return 0

    def scatter(p, _):
        base = p * (SPANS * SLOT) + c * SLOT

        def group(g, _):
            wanted = [ids[base + g * UNROLL + j] for j in range(UNROLL)]
            add_rows(([total, other], wanted, staged(stage, p * (SLOT // UNROLL) + g)))
            return 0

        lax.fori_loop(0, SLOT // UNROLL, group, 0)
        return 0

    for k, back_ref in enumerate(backs):

        @pl.when((c >= BOUNDS[k]) & (c < BOUNDS[k + 1]))
        def _():
            lax.fori_loop(0, PEERS, functools.partial(unpack, back_ref), 0, unroll=4)

    lax.fori_loop(0, PEERS, scatter, 0)

    @pl.when(c == SPANS - 1)
    def _():
        table.wait()
        adagrad_tables([total, other], right_t, state, new_ref, new_state)


def right_update(ids, backs, grad, right_t, state):
    def part(k):
        return pl.BlockSpec(
            (PEERS, WIRE, 128),
            lambda c: (0, jnp.clip(c - BOUNDS[k], 0, BOUNDS[k + 1] - BOUNDS[k] - 1), 0),
        )

    vmem = pl.BlockSpec(memory_space=pltpu.VMEM)
    return pl.pallas_call(
        right_kernel,
        grid=(SPANS,),
        out_shape=[
            jax.ShapeDtypeStruct((WIDTH, ROWS), F32),
            jax.ShapeDtypeStruct((1, ROWS), F32),
        ],
        in_specs=[
            pl.BlockSpec(memory_space=pltpu.SMEM),
            *(part(k) for k in range(PARTS)),
            pl.BlockSpec(memory_space=pl.ANY),
            pl.BlockSpec(memory_space=pl.ANY),
            vmem,
        ],
        out_specs=[vmem] * 2,
        scratch_shapes=[
            pltpu.VMEM((TALL, 128), F32),
            pltpu.VMEM((TALL, 128), F32),
            pltpu.VMEM((PEERS * 4 * SLOT, 128), F32),
            pltpu.SemaphoreType.DMA,
            pltpu.VMEM((WIDTH, ROWS), F32),
            pltpu.SemaphoreType.DMA,
        ],
        compiler_params=pltpu.CompilerParams(**PARAMS),
        cost_estimate=pl.CostEstimate(flops=0, bytes_accessed=4_000_000, transcendentals=0),
        name="right_update",
    )(ids, *backs, grad, right_t, state)


def places():
    grp, shard = lax.axis_index("grp"), lax.axis_index("shard")
    core, chip = lax.rem(grp, CORES), lax.div(grp, CORES)

    def other_core():
        return (chip * CORES + 1 - core, shard)

    def along_grp(d):
        return (lax.rem(chip + d, CHIPS) * CORES + core, shard)

    def along_shard(d):
        return (grp, lax.rem(shard + d, PEERS))

    return core, chip, shard, other_core, along_grp, along_shard


def greet(devices):
    barrier = pltpu.get_barrier_semaphore()
    for device in devices:
        pl.semaphore_signal(
            barrier, inc=1, device_id=device, device_id_type=pl.DeviceIdType.MESH
        )
    pl.semaphore_wait(barrier, len(devices))


def sender(sends, recvs):
    def send(src, dst, slot, to):
        copy = pltpu.make_async_remote_copy(
            src_ref=src, dst_ref=dst, send_sem=sends.at[slot], recv_sem=recvs.at[slot],
            device_id=to, device_id_type=pl.DeviceIdType.MESH,
        )
        copy.start()
        return copy

    return send


def relation_sum_kernel(mine, out, got_0, half, got_1, sum_1, got_2, sum_2, sends, recvs):
    core, chip, shard, other_core, along_grp, along_shard = places()
    steps = range(1, PEERS)
    greet(
        [other_core()] + [along_shard(d) for d in steps] + [along_grp(d) for d in steps]
    )
    send = sender(sends, recvs)
    copy = send(mine.at[1 - core], got_0, 0, other_core())
    copy.wait()

    def add(p, _):
        half[p] = (mine[core, p].astype(F32) + got_0[p].astype(F32)).astype(BF16)
        return 0

    lax.fori_loop(0, PEERS, add, 0)
    copies = [
        send(half.at[lax.rem(shard + d, PEERS)], got_1.at[d - 1], d, along_shard(d))
        for d in steps
    ]
    for copy in copies:
        copy.wait()

    def total_of(k, _):
        total = mine[core, shard, k].astype(F32) + got_0[shard, k].astype(F32)
        for d in range(PEERS - 1):
            total = total + got_1[d, k].astype(F32)
        sum_1[k] = total
        return 0

    lax.fori_loop(0, CHIPS, total_of, 0)
    copies = [
        send(sum_1.at[lax.rem(chip + d, CHIPS)], got_2.at[d - 1], 7 + d, along_grp(d))
        for d in steps
    ]
    for copy in copies:
        copy.wait()
    total = sum_1[chip]
    for d in range(CHIPS - 1):
        total = total + got_2[d]
    sum_2[...] = total
    out[chip] = total
    copies = [send(sum_2, out.at[chip], 14 + d, along_grp(d)) for d in steps]
    for copy in copies:
        copy.wait()


def relation_sum(grad):
    vmem = pl.BlockSpec(memory_space=pltpu.VMEM)
    return pl.pallas_call(
        relation_sum_kernel,
        out_shape=jax.ShapeDtypeStruct((CHIPS, REL_SHARE, 128), F32),
        in_specs=[vmem],
        out_specs=vmem,
        scratch_shapes=[
            pltpu.VMEM((PEERS, CHIPS, REL_SHARE, 128), BF16),
            pltpu.VMEM((PEERS, CHIPS, REL_SHARE, 128), BF16),
            pltpu.VMEM((PEERS - 1, CHIPS, REL_SHARE, 128), BF16),
            pltpu.VMEM((CHIPS, REL_SHARE, 128), F32),
            pltpu.VMEM((CHIPS - 1, REL_SHARE, 128), F32),
            pltpu.VMEM((REL_SHARE, 128), F32),
            pltpu.SemaphoreType.DMA((22,)),
            pltpu.SemaphoreType.DMA((22,)),
        ],
        compiler_params=pltpu.CompilerParams(
            collective_id=0, has_side_effects=True, vmem_limit_bytes=32 * 1024 * 1024
        ),
        cost_estimate=pl.CostEstimate(flops=0, bytes_accessed=4_000_000, transcendentals=0),
        name="relation_sum",
    )(grad.reshape(CORES, PEERS, CHIPS, REL_SHARE, 128))


def relation_spread_kernel(mine, out, sends, recvs):
    core, chip, shard, other_core, along_grp, along_shard = places()
    steps = range(1, PEERS)
    greet([other_core()] + [along_shard(d) for d in steps])
    send = sender(sends, recvs)
    copies = [send(mine, out.at[core, shard], d, along_shard(d)) for d in steps]
    out[core, shard] = mine[...]
    across = [send(mine, out.at[core, shard], 8, other_core())]
    for d in steps:
        copies[d - 1].wait_recv()
        block = out.at[core, lax.rem(shard + PEERS - d, PEERS)]
        across.append(send(block, block, 8 + d, other_core()))
    for copy in copies:
        copy.wait_send()
    for copy in across:
        copy.wait()


def relation_spread(total):
    vmem = pl.BlockSpec(memory_space=pltpu.VMEM)
    out = pl.pallas_call(
        relation_spread_kernel,
        out_shape=jax.ShapeDtypeStruct((CORES, PEERS, CHIPS, REL_SHARE, 128), F32),
        in_specs=[vmem],
        out_specs=vmem,
        scratch_shapes=[pltpu.SemaphoreType.DMA((16,)), pltpu.SemaphoreType.DMA((16,))],
        compiler_params=pltpu.CompilerParams(
            collective_id=1, has_side_effects=True, vmem_limit_bytes=32 * 1024 * 1024
        ),
        cost_estimate=pl.CostEstimate(flops=0, bytes_accessed=4_000_000, transcendentals=0),
        name="relation_spread",
    )(total)
    return out.reshape(REL_TALL, 128)


def relation_kernel(g_ref, rel_t, state, new_ref, new_state):
    for i in range(RELS_PAD // 128):
        low, high = i * 128, min(RELS, i * 128 + 128)
        new, ns = adagrad_block([g_ref], rel_t[:, low : low + 128], state[:, low : low + 128], i)
        new_ref[:, low:high] = new[:, : high - low]
        new_state[:, low:high] = ns[:, : high - low]


def relation_update(grad, rel_t, state):
    vmem = pl.BlockSpec(memory_space=pltpu.VMEM)
    return pl.pallas_call(
        relation_kernel,
        out_shape=[
            jax.ShapeDtypeStruct((WIDTH, RELS), F32),
            jax.ShapeDtypeStruct((1, RELS), F32),
        ],
        in_specs=[vmem] * 3,
        out_specs=[vmem] * 2,
        compiler_params=pltpu.CompilerParams(**PARAMS),
        name="relation_update",
    )(grad, rel_t, state)


def passed_along(block, axis, distance):
    devices = range(lax.axis_size(axis))
    route = [((i - distance) % len(devices), i) for i in devices]
    return lax.ppermute(block, axis, route)


def exchange(x):
    return lax.all_to_all(x, "shard", split_axis=0, concat_axis=0, tiled=True)


def local(
    left_table, right_table, left_state, right_state, relations, relation_state,
    source_rows, relation_ids, target_rows, negative_rows, span_sizes,
):
    left_t, right_t = left_table.T, right_table.T
    wanted = negative_rows.reshape(SPANS, PEERS, NEG_PER).transpose(1, 0, 2)
    wanted = jnp.pad(wanted, ((0, 0), (0, 0), (0, SLOT - NEG_PER)), constant_values=DUMP)
    asked = exchange(wanted.reshape(PEERS, SPANS * SLOT)).reshape(-1)
    served = serve(asked, right_t)
    got = exchange(served)

    def flat(ids):
        return jnp.pad(ids, ((0, 0), (0, SPAN_PAD - ids.shape[1]))).reshape(-1)

    src, rel, tgt = flat(source_rows), flat(relation_ids), flat(target_rows)
    live = span_sizes.reshape(SPANS)
    rel_t = jnp.pad(relations.T, ((0, 0), (0, RELS_PAD - RELS)))
    rel_state = jnp.pad(relation_state, (0, RELS_PAD - RELS), constant_values=1.0)
    source, relation, product, pos_target, grad_right = forward(
        src, rel, tgt, live, left_t, right_t, rel_t
    )
    grad_product, returned = None, []
    for first, end in zip(BOUNDS, BOUNDS[1:]):
        grad_product, back = negatives(
            live, product, pos_target, got, first, end - first, grad_product
        )
        if returned:
            returned[-1], back = lax.optimization_barrier((returned[-1], back))
        returned.append(exchange(back))
    new_left, new_left_state, grad_rel = left_update(
        src, rel, live, source, relation, grad_product, left_t, left_state.reshape(1, ROWS)
    )
    moved_left = passed_along(new_left.astype(jnp.float16), "grp", ROUND)
    new_right, new_right_state = right_update(
        asked, returned, grad_right, right_t, right_state.reshape(1, ROWS)
    )
    grad_rel, sent = lax.optimization_barrier((grad_rel, new_right.astype(jnp.float16)))
    rel_share = relation_sum(grad_rel)
    rel_share, sent = lax.optimization_barrier((rel_share, sent))
    moved_right = passed_along(sent, "grp", ROUND)
    rel_total = relation_spread(rel_share)
    states = jnp.concatenate([new_left_state, new_right_state], 0)
    moved_states = passed_along(states, "grp", ROUND)
    held_left, rel_total = lax.optimization_barrier((moved_left.astype(F32), rel_total))
    new_rel, new_rel_state = relation_update(rel_total, rel_t, rel_state.reshape(1, RELS_PAD))
    moved_right, moved_states, new_rel = lax.optimization_barrier(
        (moved_right, moved_states, new_rel)
    )
    return (
        held_left.T,
        moved_states[0],
        moved_right.astype(F32).T,
        moved_states[1],
        new_rel.T,
        new_rel_state.reshape(RELS),
    )


def solution(mesh):
    rows, flat = P(("grp", "shard"), None), P(("grp", "shard"))
    return jax.shard_map(
        local,
        mesh=mesh,
        in_specs=(rows, rows, flat, flat, P(), P(), rows, rows, rows, rows, rows),
        out_specs=(rows, flat, rows, flat, P(), P()),
        check_vma=False,
    )
```
